32 devices in a mesh: dp: 8 (over z, y), blk: 4 (over x, core).
Axes of the slice: x: 2, y: 2, z: 4, core: 2. Of those that a mesh axis runs over, the one named last changes fastest.
Arguments:
- programs: float32 [4096, 512], P(('dp', 'blk'))
- traces: float32 [4096, 512], P(('dp', 'blk'))
- hard_owner: int32 [4096, 16], P(('dp', 'blk')), may hold values from 0 to 31, all different within a row; in each aligned block of 128 rows (0 to 127, 128 to 255, ...) at most 96 rows name the same one
- hard_row: int32 [4096, 16], P(('dp', 'blk')), may hold values from 0 to 127
Outputs:
- grad_programs: float32 [4096, 512], P(('dp', 'blk'))
- grad_traces: float32 [4096, 512], P(('dp', 'blk'))
- row_loss: float32 [4096], P(('dp', 'blk'))
The draws below stay inside these ranges and needn't reach their ends.
Inputs may be any that keep to these rules, and one draw needn't show every extreme that they name: `hard_owner`: each program names 16 different blocks. Among the 128 programs of one device at most 96 name the same block, and in every draw some device has a block named by exactly 96 of its programs.
All inputs are finite; a program needn't handle non-finite values.
Results may differ from the reference program's by a relative error of at most 0.00035.
Values may be sent and summed in bfloat16 or wider, within the bound.
No kernel may reach another device: no remote copies, remote signals or barrier semaphores. Data moves between devices by JAX's collectives and lax.ppermute only.
A program may use at most 64 MiB of HBM per device.

```python
import math
import jax
import jax.numpy as jnp
import numpy as np
from jax import lax

D = 512
NEG = 16
ROWS_DEV = 128
PAIRS = 4096
CAP = 96
N_DP = 8
N_BLK = 4


def pair_fields(key):
    key_base = jax.random.fold_in(key, 101)
    key_noise = jax.random.fold_in(key, 102)
    base = jax.random.normal(key_base, (PAIRS, D), jnp.float32)
    noise = jax.random.normal(key_noise, (PAIRS, D), jnp.float32)
    factor = 1.0 / math.sqrt(D)
    traces = base * factor
    programs = (0.35 * base + noise) * factor
    return (programs, traces)


def draw_programs(key, part):
    return pair_fields(key)[0].astype(jnp.float32)


def draw_traces(key, part):
    return pair_fields(key)[1].astype(jnp.float32)


def touch_ends(array, stream_key, low, largest):
    longest = array.shape.index(max(array.shape))
    spots = []
    for shift in (0, 1):
        where = [jax.random.randint(jax.random.fold_in(stream_key, axis), (), 0, length) for axis, length in enumerate(array.shape)]
        where[longest] = (where[longest] + shift) % array.shape[longest]
        spots.append(tuple(where))
    return array.at[spots[0]].set(low).at[spots[1]].set(largest)


def shared_out(stream_key, own, number, rows, number_of, top, bound, skew):
    ranking = jax.random.permutation(stream_key, number_of)
    heavy_load, usual = load_shares(number_of, rows * top, bound, skew, True), load_shares(number_of, rows * top, bound, skew, False)
    places = jnp.arange(number_of)

    def named(lengths, turn):
        used = int((lengths > 0).sum())
        fixed = max(1, used // 4)
        passed = fixed + (places - fixed + turn * (used - fixed)) % max(1, number_of - fixed)
        return jnp.zeros((number_of,), jnp.int32).at[ranking[jnp.where(places < fixed, places, passed)]].set(jnp.asarray(lengths, jnp.int32))

    lengths = jnp.where(number % 4 == 0, named(heavy_load, number // 4), named(usual, number - number // 4 - 1))
    mixed = jax.random.permutation(jax.random.fold_in(own, 3), number_of)
    donor, sink = mixed[0:number_of // 2 * 2:2], mixed[1:number_of // 2 * 2:2]
    slack = jnp.minimum(lengths[donor] - 1, bound - lengths[sink]) // 2
    slack = jnp.where((donor == ranking[0]) | (sink == ranking[0]) | (lengths[sink] == 0), 0, jnp.maximum(slack, 0))
    passed = jax.random.randint(jax.random.fold_in(own, 4), (number_of // 2,), 0, 1 << 20) % (slack + 1)
    lengths = lengths.at[donor].add(-passed).at[sink].add(passed)
    members = jnp.searchsorted(jnp.cumsum(lengths), jnp.arange(rows * top), side="right").astype(jnp.int32)
    grid = members.reshape(top, rows).T
    grid = grid[jax.random.permutation(jax.random.fold_in(own, 1), rows)]
    turn = jax.random.randint(jax.random.fold_in(own, 2), (rows, 1), 0, top)
    return jnp.take_along_axis(grid, (jnp.arange(top)[None, :] + turn) % top, axis=1)


def load_shares(number_of, total, bound, slope, full):
    portions = [(1 << 20) // math.isqrt(standing ** slope) + 1 for standing in range(1, number_of + 1)]
    largest = bound if full else min(bound, max(-(-total // number_of), total * portions[0] // sum(portions)))
    least = 1 if total - largest >= number_of - 1 else 0
    given, spare = [largest] + [least] * (number_of - 1), total - largest - least * (number_of - 1)
    while spare > 0:
        movable = [i for i in range(1, number_of) if given[i] < largest] or [i for i in range(1, number_of) if given[i] < bound]
        pool, remaining = sum([portions[i] for i in movable]), spare
        for i in movable:
            more = min(bound - given[i], max(1, remaining * portions[i] // pool), spare)
            given[i] = given[i] + more
            spare = spare - more
    return np.array(given)


def setup_inputs(seed: int = 0) -> dict:
    arg_keys = jax.random.split(jax.random.key(seed), 5)
    programs = draw_programs(jax.random.fold_in(arg_keys[4], 71), 0)
    traces = draw_traces(jax.random.fold_in(arg_keys[4], 71), 0)
    hard_owner_keys = jax.random.split(jax.random.fold_in(arg_keys[2], 1), PAIRS // ROWS_DEV)
    hard_owner_turns = jax.random.permutation(jax.random.fold_in(arg_keys[2], 3), PAIRS // ROWS_DEV)
    hard_owner = jax.vmap(lambda own, number: shared_out(jax.random.fold_in(arg_keys[2], 2), own, number, ROWS_DEV, N_DP * N_BLK, NEG, CAP, 2))(hard_owner_keys, hard_owner_turns).reshape((PAIRS, NEG))
    hard_row = touch_ends(jax.random.randint(arg_keys[3], (PAIRS, NEG), 0, ROWS_DEV), jax.random.fold_in(arg_keys[3], 1), 0, ROWS_DEV - 1).astype(jnp.int32)
    return dict(programs=programs, traces=traces, hard_owner=hard_owner, hard_row=hard_row)


EPSILON = 1e-06
LOGIT_SCALE = 14.0
HIGH = lax.Precision.HIGHEST

def normalize(values):
    length = jnp.sqrt(lax.optimization_barrier(jnp.sum(values * values, axis=-1, keepdims=True)) + EPSILON)
    return (values / length, length)

def group_terms(blocks):
    prog_block, trace_block = blocks
    scores = LOGIT_SCALE * jnp.einsum('rd,cd->rc', prog_block, trace_block, precision=HIGH, preferred_element_type=jnp.float32)
    log_total = jnp.log(lax.optimization_barrier(jnp.sum(jnp.exp(scores), axis=1)))
    weights = jnp.exp(scores - log_total[:, None])
    prog_grad = LOGIT_SCALE * jnp.dot(weights, trace_block, precision=HIGH, preferred_element_type=jnp.float32)
    trace_grad = LOGIT_SCALE * jnp.einsum('rc,rd->cd', weights, prog_block, precision=HIGH, preferred_element_type=jnp.float32)
    return (log_total, prog_grad, trace_grad)

def reference(programs, traces, hard_owner, hard_row):
    prog_unit, prog_len = normalize(programs)
    trace_unit, trace_len = normalize(traces)
    group_rows = N_BLK * ROWS_DEV
    log_group, grad_prog, grad_trace = lax.map(group_terms, (prog_unit.reshape(N_DP, group_rows, D), trace_unit.reshape(N_DP, group_rows, D)))
    log_group = log_group.reshape(PAIRS)
    grad_prog = grad_prog.reshape(PAIRS, D)
    grad_trace = grad_trace.reshape(PAIRS, D)
    trace_low = trace_unit.astype(jnp.bfloat16)
    targets = (hard_owner.astype(jnp.int32) * ROWS_DEV + hard_row.astype(jnp.int32)).astype(jnp.int32)
    blocks = N_DP * N_BLK

    def hard_step(carry, pieces):
        prog_block, trace_block, target_block = pieces
        fetched = trace_low[target_block].astype(jnp.float32)
        hard_scores = LOGIT_SCALE * jnp.einsum('rd,rnd->rn', prog_block, fetched, precision=HIGH)
        pos_score = LOGIT_SCALE * lax.optimization_barrier(jnp.sum(prog_block * trace_block, axis=-1))
        log_hard = jnp.log(jnp.exp(pos_score) + lax.optimization_barrier(jnp.sum(jnp.exp(hard_scores), axis=1)))
        hard_weight = jnp.exp(hard_scores - log_hard[:, None])
        pos_weight = jnp.exp(pos_score - log_hard)
        prog_term = LOGIT_SCALE * (jnp.einsum('rn,rnd->rd', hard_weight, fetched, precision=HIGH) + (pos_weight - 2.0)[:, None] * trace_block)
        trace_term = LOGIT_SCALE * (pos_weight - 2.0)[:, None] * prog_block
        sent = (LOGIT_SCALE * hard_weight[:, :, None] * prog_block[:, None, :]).astype(jnp.bfloat16)
        sent = lax.optimization_barrier(sent).astype(jnp.float32)
        carry = carry.at[target_block.reshape(-1)].add(sent.reshape(-1, D))
        return (carry, (log_hard - 2.0 * pos_score, prog_term, trace_term))
    start_grad = jnp.zeros((PAIRS, D), jnp.float32)
    grad_back, outputs = lax.scan(hard_step, start_grad, (prog_unit.reshape(blocks, ROWS_DEV, D), trace_unit.reshape(blocks, ROWS_DEV, D), targets.reshape(blocks, ROWS_DEV, NEG)))
    loss_part, prog_hard, trace_hard = outputs
    row_loss = log_group + loss_part.reshape(PAIRS)
    dir_prog = grad_prog + prog_hard.reshape(PAIRS, D)
    dir_trace = grad_trace + grad_back + trace_hard.reshape(PAIRS, D)
    grad_programs = (dir_prog - prog_unit * lax.optimization_barrier(jnp.sum(prog_unit * dir_prog, axis=-1, keepdims=True))) / prog_len
    grad_traces = (dir_trace - trace_unit * lax.optimization_barrier(jnp.sum(trace_unit * dir_trace, axis=-1, keepdims=True))) / trace_len
    return (grad_programs, grad_traces, row_loss)
```

```python
import functools

import jax
import jax.numpy as jnp
from jax import lax
from jax.experimental import pallas as pl
from jax.experimental.pallas import tpu as pltpu
from jax.sharding import PartitionSpec as P

EPSILON = 1e-06
SCALE = 14.0
LOW = jnp.bfloat16
F32 = jnp.float32
ROWS = 128
VMEM_LIMIT = 40 * 1024 * 1024


def normalize(values):
    length = jnp.sqrt(jnp.sum(values * values, axis=-1, keepdims=True) + EPSILON)
    return values / length, length


def dot(a, b, contract=(1, 0)):
    return lax.dot_general(
        a, b, (((contract[0],), (contract[1],)), ((), ())), preferred_element_type=F32
    )


def halves(values):
    high = values.astype(LOW)
    return high, (values - high.astype(F32)).astype(LOW)


def dot3(a, b, contract=(1, 0)):
    return (
        dot(a[0], b[1], contract) + dot(a[1], b[0], contract)
    ) + dot(a[0], b[0], contract)


def eye():
    shape = (ROWS, ROWS)
    return lax.broadcasted_iota(jnp.int32, shape, 0) == lax.broadcasted_iota(jnp.int32, shape, 1)


def to_row(column):
    return jnp.sum(jnp.where(eye(), column, 0.0), axis=0, keepdims=True)


def to_column(row):
    return jnp.sum(jnp.where(eye(), row, 0.0), axis=1, keepdims=True)


def own_plane():
    return lax.div(lax.axis_index("dp"), 2)


def own_core():
    return lax.rem(lax.axis_index("blk"), 2)


def aux_rows(planes, feat):
    per_row = feat // ROWS
    picks = 8 * (-(-planes // per_row))
    return picks, -(-(picks + 8) // 16) * 16


def prepare(planes, prog_ref, trace_ref, owner_ref, row_ref, msg_ref, low_ref, group_ref):
    feat = prog_ref.shape[1]
    neg = owner_ref.shape[1]
    prog_unit, _ = normalize(prog_ref[...])
    trace_unit, _ = normalize(trace_ref[...])
    prog_high, prog_low = halves(prog_unit)
    trace_high, trace_low = halves(trace_unit)
    msg_ref[0:ROWS, :] = prog_high
    low_ref[...] = trace_high
    group_ref[0:ROWS, :] = trace_low
    group_ref[ROWS : 2 * ROWS, :] = prog_high
    group_ref[2 * ROWS : 3 * ROWS, :] = prog_low
    pos = to_row(SCALE * jnp.sum(prog_unit * trace_unit, axis=-1, keepdims=True))
    unit = jnp.where(eye(), 1.0, 0.0).astype(LOW)
    owners = dot(owner_ref[...].astype(F32).astype(LOW), unit, (0, 0))
    rows = dot(row_ref[...].astype(F32).astype(LOW), unit, (0, 0)) + 1.0
    index = lax.broadcasted_iota(jnp.int32, (planes * 8, ROWS), 0).astype(F32)
    picks = jnp.zeros((planes * 8, ROWS), F32)
    for n in range(neg):
        picks = picks + jnp.where(index == owners[n : n + 1, :], rows[n : n + 1, :], 0.0)
    per_row = feat // ROWS
    blank = jnp.zeros((8, ROWS), F32)
    parts = []
    for start in range(0, planes, per_row):
        tiles = [
            picks[p * 8 : p * 8 + 8, :] if p < planes else blank
            for p in range(start, start + per_row)
        ]
        parts.append(jnp.concatenate(tiles, axis=1))
    high = pos.astype(LOW).astype(F32)
    mid = (pos - high).astype(LOW).astype(F32)
    last = pos - high - mid
    line = lax.broadcasted_iota(jnp.int32, (8, ROWS), 0)
    pos_tile = jnp.where(line == 0, high, jnp.where(line == 1, mid, jnp.where(line == 2, last, 0.0)))
    parts.append(jnp.concatenate([pos_tile] + [blank] * (per_row - 1), axis=1))
    left = msg_ref.shape[0] - ROWS - 8 * len(parts)
    if left:
        parts.append(jnp.zeros((left, feat), F32))
    msg_ref[ROWS:, :] = jnp.concatenate(parts, axis=0).astype(LOW)


def score(planes, *refs):
    count = 2 * planes
    msgs, traces = refs[:count], refs[count : count + 8]
    exp_ref, pick_ref, sum_ref, pos_ref, prog_ref, trace_ref = refs[count + 8 :]
    feat = trace_ref.shape[1]
    per_row = feat // ROWS
    picks_rows, _ = aux_rows(planes, feat)
    plane, core = own_plane(), own_core()
    for b, msg in enumerate(msgs):
        prog_ref[b * ROWS : (b + 1) * ROWS, :] = msg[0:ROWS, :]
        aux = msg[ROWS:, :].astype(F32)
        chosen = jnp.zeros((8, ROWS), F32)
        for p in range(planes):
            at, lane = 8 * (p // per_row), ROWS * (p % per_row)
            tile = aux[at : at + 8, lane : lane + ROWS]
            chosen = chosen + jnp.where(plane == p, 1.0, 0.0) * tile
        pick_ref[:, b * ROWS : (b + 1) * ROWS] = by_slot(chosen)
        pos = aux[picks_rows : picks_rows + 8, 0:ROWS]
        pos_ref[:, b * ROWS : (b + 1) * ROWS] = pos[0:1, :] + pos[1:2, :] + pos[2:3, :]
    for q in range(8):
        trace_ref[q * ROWS : (q + 1) * ROWS, :] = traces[q][...]
    total_width = count * ROWS
    below = lax.broadcasted_iota(jnp.int32, (ROWS, total_width), 0).astype(F32) + 1.0
    sums = jnp.zeros((1, total_width), F32)
    for q in range(8):
        scores = dot(traces[q][...], prog_ref[...], (1, 1))
        pick = pick_ref[q : q + 1, :]
        found = jnp.sum(jnp.where(below == pick, scores, 0.0), axis=0, keepdims=True)
        exps = jnp.where(pick > 0.0, jnp.exp(SCALE * found), 0.0)
        exp_ref[q : q + 1, :] = exps
        sums = sums + exps
    for b in range(count):
        sum_ref[:, pl.ds(block_lane(planes, b, plane, core), ROWS)] = sums[
            :, b * ROWS : (b + 1) * ROWS
        ]


def by_slot(picks):
    blk = lax.axis_index("blk")
    bits = (lax.rem(blk, 2), lax.div(blk, 2), lax.rem(lax.axis_index("dp"), 2))
    for step, bit in zip((1, 2, 4), bits):
        turned = []
        for at in range(0, 8, 2 * step):
            turned += [picks[at + step : at + 2 * step, :], picks[at : at + step, :]]
        picks = jnp.where(bit == 1, jnp.concatenate(turned, axis=0), picks)
    return picks


def block_lane(planes, b, plane, core):
    source = lax.rem(plane - b % planes + planes, planes)
    other = core if b < planes else 1 - core
    return pl.multiple_of((2 * source + other) * ROWS, ROWS)


def program_terms(planes, exp_ref, pick_ref, trace_ref, own_ref, *out_refs):
    width = planes * ROWS
    lanes = lax.broadcasted_iota(jnp.int32, (width, ROWS), 1).astype(F32) + 1.0
    exps = jnp.transpose(exp_ref[:, 0:width])
    picks = jnp.transpose(pick_ref[:, 0:width])
    high, low = [], []
    for q in range(8):
        values = jnp.where(lanes == picks[:, q : q + 1], exps[:, q : q + 1], 0.0)
        value_high, value_low = halves(values)
        high.append(value_high)
        low.append(value_low)
    total = dot(jnp.concatenate(high, axis=1), trace_ref[...]) + dot(
        jnp.concatenate(low, axis=1), trace_ref[...]
    )
    own_ref[...] = total[0:ROWS, :]
    for k, out_ref in enumerate(out_refs, 1):
        out_ref[...] = total[k * ROWS : (k + 1) * ROWS, :].astype(LOW)


def trace_terms(planes, exp_ref, pick_ref, pos_ref, prog_ref, *refs):
    sums = refs[:planes]
    total_ref, own_ref, x_ref, y_ref, xy_ref = refs[planes : planes + 5]
    high_ref, low_ref = refs[planes + 5 :]
    plane, core = own_plane(), own_core()
    count = 2 * planes
    below = lax.broadcasted_iota(jnp.int32, (ROWS, ROWS), 0).astype(F32) + 1.0
    for b in range(count):
        lane = block_lane(planes, b, plane, core)
        total = jnp.exp(pos_ref[:, b * ROWS : (b + 1) * ROWS])
        for one in sums:
            total = total + one[:, pl.ds(lane, ROWS)]
        if b == 0:
            total_ref[...] = total
        scale = SCALE / total
        for i in range(4):
            q = 2 * i
            weight = exp_ref[q : q + 1, b * ROWS : (b + 1) * ROWS] * scale
            pick = pick_ref[q : q + 1, b * ROWS : (b + 1) * ROWS]
            values = jnp.where(below == pick, weight, 0.0)
            high, low = halves(values)
            high_ref[i * ROWS : (i + 1) * ROWS, b * ROWS : (b + 1) * ROWS] = high
            low_ref[i * ROWS : (i + 1) * ROWS, b * ROWS : (b + 1) * ROWS] = low
    result = dot(high_ref[...], prog_ref[...]) + dot(low_ref[...], prog_ref[...])
    own_ref[...] = result[0:ROWS, :]
    for i, out_ref in enumerate((x_ref, y_ref, xy_ref), 1):
        out_ref[...] = result[i * ROWS : (i + 1) * ROWS, :].astype(LOW)


def group_terms(*refs):
    highs, groups = refs[:4], refs[4:8]
    prog_out, trace_out, log_ref = refs[8:]

    def joined(parts):
        return jnp.concatenate(parts, axis=0)

    trace = (joined([h[...] for h in highs]), joined([g[0:ROWS, :] for g in groups]))
    prog = (
        joined([g[ROWS : 2 * ROWS, :] for g in groups]),
        joined([g[2 * ROWS :, :] for g in groups]),
    )
    scores = SCALE * dot3(prog, trace, (1, 1))
    exps = jnp.exp(scores)
    total = jnp.sum(exps, axis=1, keepdims=True)
    weights = exps / total
    log_ref[...] = to_row(jnp.log(total[0:ROWS, :]))
    prog_out[...] = dot3(halves(weights[0:ROWS, :]), trace)
    trace_out[...] = dot3(halves(jnp.transpose(weights[:, 0:ROWS])), prog)


def finish(planes, prog_ref, trace_ref, total_ref, log_ref, group_prog, group_trace, *refs):
    prog_own, progs = refs[0], refs[1:planes]
    trace_own, traces = refs[planes], refs[planes + 1 : planes + 4]
    grad_prog_ref, grad_trace_ref, loss_ref = refs[planes + 4 :]
    prog_unit, prog_len = normalize(prog_ref[...])
    trace_unit, trace_len = normalize(trace_ref[...])
    pos = SCALE * jnp.sum(prog_unit * trace_unit, axis=-1, keepdims=True)
    total = to_column(total_ref[...])
    hard = prog_own[...]
    for one in progs:
        hard = hard + one[...].astype(F32)
    pull = jnp.exp(pos) / total - 2.0
    dir_prog = SCALE * (group_prog[...] + hard / total + pull * trace_unit)
    back = trace_own[...]
    for one in traces:
        back = back + one[...].astype(F32)
    dir_trace = SCALE * (group_trace[...] + pull * prog_unit) + back
    along = jnp.sum(prog_unit * dir_prog, axis=-1, keepdims=True)
    grad_prog_ref[...] = (dir_prog - prog_unit * along) / prog_len
    along = jnp.sum(trace_unit * dir_trace, axis=-1, keepdims=True)
    grad_trace_ref[...] = (dir_trace - trace_unit * along) / trace_len
    loss_ref[...] = log_ref[...] + (jnp.log(total_ref[...]) - 2.0 * to_row(pos))


def call(body, outs, flops, moved, scratch=()):
    return pl.pallas_call(
        body,
        out_shape=[jax.ShapeDtypeStruct(shape, dtype) for shape, dtype in outs],
        scratch_shapes=list(scratch),
        compiler_params=pltpu.CompilerParams(vmem_limit_bytes=VMEM_LIMIT),
        cost_estimate=pl.CostEstimate(flops=flops, bytes_accessed=moved, transcendentals=0),
    )


def on_device(dp_count, blk_count, programs, traces, hard_owner, hard_row):
    rows, feat = programs.shape
    planes = dp_count // 2
    size = dp_count * blk_count
    both = ("dp", "blk")

    def flipped(value, bits):
        return lax.ppermute(value, both, [(i, i ^ bits) for i in range(size)])

    def shifted(value, by):
        plane_size = 2 * blk_count
        return lax.ppermute(
            value, both, [(i, (i + by * plane_size) % size) for i in range(size)]
        )

    x_bit, y_bit = 2, blk_count
    _, extra = aux_rows(planes, feat)
    block = rows * feat
    msg, high, group = call(
        functools.partial(prepare, planes),
        [((rows + extra, feat), LOW), ((rows, feat), LOW), ((3 * rows, feat), LOW)],
        10 * block,
        20 * block,
    )(programs, traces, hard_owner, hard_row)

    msgs = [msg] + [shifted(msg, k) for k in range(1, planes)]
    highs = [high, flipped(high, x_bit), flipped(high, y_bit), flipped(high, x_bit + y_bit)]
    other_highs = [flipped(one, 1) for one in highs]
    other_msgs = [flipped(one, 1) for one in msgs]
    slots = [one for pair in zip(highs, other_highs) for one in pair]
    group_x = flipped(group, x_bit)
    groups = [group, flipped(group, 1), group_x, flipped(group_x, 1)]

    width = 2 * planes * rows
    exps, picks, sums, pos, prog_all, trace_all = call(
        functools.partial(score, planes),
        [
            ((8, width), F32),
            ((8, width), F32),
            ((1, width), F32),
            ((1, width), F32),
            ((width, feat), LOW),
            ((8 * rows, feat), LOW),
        ],
        2 * 8 * rows * width * feat,
        4 * width * feat,
    )(*msgs, *other_msgs, *slots)
    all_sums = [sums] + [shifted(sums, k) for k in range(1, planes)]

    prog_parts = call(
        functools.partial(program_terms, planes),
        [((rows, feat), F32)] + [((rows, feat), LOW)] * (planes - 1),
        4 * 8 * rows * planes * rows * feat,
        4 * width * feat,
    )(exps, picks, trace_all)
    prog_back = [prog_parts[0]] + [shifted(prog_parts[k], -k) for k in range(1, planes)]

    total, trace_own, part_x, part_y, part_xy = call(
        functools.partial(trace_terms, planes),
        [((1, rows), F32), ((rows, feat), F32)] + [((rows, feat), LOW)] * 3,
        4 * 4 * rows * width * feat,
        4 * width * feat,
        [pltpu.VMEM((4 * rows, width), LOW)] * 2,
    )(exps, picks, pos, prog_all, *all_sums)
    trace_back = [
        trace_own,
        flipped(part_x, x_bit),
        flipped(part_y, y_bit),
        flipped(part_xy, x_bit + y_bit),
    ]

    group_prog, group_trace, log_group = call(
        group_terms,
        [((rows, feat), F32), ((rows, feat), F32), ((1, rows), F32)],
        6 * 6 * rows * 4 * rows * feat,
        20 * block,
    )(*slots[:4], *groups)

    grad_programs, grad_traces, loss = call(
        functools.partial(finish, planes),
        [((rows, feat), F32), ((rows, feat), F32), ((1, rows), F32)],
        20 * block,
        30 * block,
    )(
        programs,
        traces,
        total,
        log_group,
        group_prog,
        group_trace,
        *prog_back,
        *trace_back,
    )
    return grad_programs, grad_traces, loss.reshape(rows)


def solution(mesh):
    spec = P(("dp", "blk"), None)
    return jax.shard_map(
        functools.partial(on_device, mesh.shape["dp"], mesh.shape["blk"]),
        mesh=mesh,
        in_specs=(spec,) * 4,
        out_specs=(spec, spec, P(("dp", "blk"))),
        check_vma=False,
    )
```

```python
import functools

import jax
import jax.numpy as jnp
from jax import lax
from jax.experimental import pallas as pl
from jax.experimental.pallas import tpu as pltpu
from jax.sharding import PartitionSpec as P

EPSILON = 1e-06
SCALE = 14.0
LOW = jnp.bfloat16
F32 = jnp.float32
ROWS = 128
VMEM_LIMIT = 40 * 1024 * 1024


def normalize(values):
    length = jnp.sqrt(jnp.sum(values * values, axis=-1, keepdims=True) + EPSILON)
    return values / length, length


def dot(a, b, contract=(1, 0)):
    return lax.dot_general(
        a, b, (((contract[0],), (contract[1],)), ((), ())), preferred_element_type=F32
    )


def halves(values):
    high = values.astype(LOW)
    return high, (values - high.astype(F32)).astype(LOW)


def dot3(a, b, contract=(1, 0)):
    return (
        dot(a[0], b[1], contract) + dot(a[1], b[0], contract)
    ) + dot(a[0], b[0], contract)


def eye():
    shape = (ROWS, ROWS)
    return lax.broadcasted_iota(jnp.int32, shape, 0) == lax.broadcasted_iota(jnp.int32, shape, 1)


def to_row(column):
    return jnp.sum(jnp.where(eye(), column, 0.0), axis=0, keepdims=True)


def to_column(row):
    return jnp.sum(jnp.where(eye(), row, 0.0), axis=1, keepdims=True)


def own_plane():
    return lax.div(lax.axis_index("dp"), 2)


def own_core():
    return lax.rem(lax.axis_index("blk"), 2)


def prepare(planes, *refs):
    sources, msg_refs, refs = refs[:4], refs[4 : 4 + planes], refs[4 + planes :]
    (high_ref, group_ref), buffers, pick_ref, sems = refs[:2], refs[2:6], refs[6], refs[7]
    copies = [
        pltpu.make_async_copy(source, buffer, sems.at[i])
        for i, (source, buffer) in enumerate(zip(sources, buffers))
    ]
    for copy in copies:
        copy.start()
    for copy in copies:
        copy.wait()
    prog_ref, trace_ref, owner_ref, row_ref = buffers
    feat = prog_ref.shape[1]
    neg = owner_ref.shape[0]
    prog_unit, _ = normalize(prog_ref[...])
    trace_unit, _ = normalize(trace_ref[...])
    prog_high, prog_low = halves(prog_unit)
    high_ref[...], group_ref[0:ROWS, :] = halves(trace_unit)
    group_ref[ROWS : 2 * ROWS, :] = prog_high
    group_ref[2 * ROWS : 3 * ROWS, :] = prog_low
    pos = to_row(SCALE * jnp.sum(prog_unit * trace_unit, axis=-1, keepdims=True))
    high = pos.astype(LOW).astype(F32)
    mid = (pos - high).astype(LOW).astype(F32)
    last = pos - high - mid
    line = lax.broadcasted_iota(jnp.int32, (8, ROWS), 0)
    pos_tile = jnp.where(line == 0, high, jnp.where(line == 1, mid, jnp.where(line == 2, last, 0.0)))
    owners = owner_ref[...]
    rows = row_ref[...].astype(F32) + 1.0
    index = lax.broadcasted_iota(jnp.int32, (planes * 8, ROWS), 0)
    picks = jnp.zeros((planes * 8, ROWS), F32)
    for n in range(neg):
        picks = picks + jnp.where(index == owners[n : n + 1, :], rows[n : n + 1, :], 0.0)
    pick_ref[...] = picks
    plane = own_plane()
    rest = jnp.zeros((8, feat - 2 * ROWS), F32)
    for k, msg_ref in enumerate(msg_refs):
        at = pl.multiple_of(8 * lax.rem(plane + k, planes), 8)
        aux = jnp.concatenate([pick_ref[pl.ds(at, 8), :], pos_tile, rest], axis=1)
        msg_ref[0:ROWS, :] = prog_high
        msg_ref[ROWS:, :] = aux.astype(LOW)


def score_block(msgs, trace_ref, exp_ref, pick_ref, pos_ref, prog_ref):
    for b, msg in enumerate(msgs):
        lanes = slice(b * ROWS, (b + 1) * ROWS)
        prog_ref[lanes, :] = msg[0:ROWS, :]
        aux = msg[ROWS:, :].astype(F32)
        pick_ref[:, lanes] = by_slot(aux[:, 0:ROWS])
        pos = aux[:, ROWS : 2 * ROWS]
        pos_ref[:, lanes] = pos[0:1, :] + pos[1:2, :] + pos[2:3, :]
    width = len(msgs) * ROWS
    below = lax.broadcasted_iota(jnp.int32, (ROWS, width), 0).astype(F32) + 1.0
    sums = jnp.zeros((1, width), F32)
    all_scores = dot(trace_ref[...], prog_ref[...], (1, 1))
    for q in range(8):
        scores = all_scores[q * ROWS : (q + 1) * ROWS, :]
        pick = pick_ref[q : q + 1, :]
        found = jnp.sum(jnp.where(below == pick, scores, 0.0), axis=0, keepdims=True)
        exps = jnp.where(pick > 0.0, jnp.exp(SCALE * found), 0.0)
        exp_ref[q : q + 1, :] = exps
        sums = sums + exps
    return sums


def score_first(own_ref, other_ref, *refs):
    traces, (exp_ref, pick_ref, pos_ref, prog_ref, sum_ref, trace_ref) = refs[:8], refs[8:]
    for q in range(8):
        trace_ref[q * ROWS : (q + 1) * ROWS, :] = traces[q][...]
    sum_ref[...] = score_block(
        (own_ref, other_ref), trace_ref, exp_ref, pick_ref, pos_ref, prog_ref
    )


def score_rest(planes, sum_in, trace_ref, *refs):
    count = 2 * planes - 2
    msgs, (exp_ref, pick_ref, pos_ref, prog_ref, sum_ref) = refs[:count], refs[count:]
    sums = score_block(msgs, trace_ref, exp_ref, pick_ref, pos_ref, prog_ref)
    plane, core = own_plane(), own_core()
    for b in range(count + 2):
        part = sum_in[:, b * ROWS : (b + 1) * ROWS] if b < 2 else sums[:, (b - 2) * ROWS : (b - 1) * ROWS]
        sum_ref[:, pl.ds(block_lane(planes, b, plane, core), ROWS)] = part


def by_slot(picks):
    blk = lax.axis_index("blk")
    bits = (lax.rem(blk, 2), lax.div(blk, 2), lax.rem(lax.axis_index("dp"), 2))
    for step, bit in zip((1, 2, 4), bits):
        turned = []
        for at in range(0, 8, 2 * step):
            turned += [picks[at + step : at + 2 * step, :], picks[at : at + step, :]]
        picks = jnp.where(bit == 1, jnp.concatenate(turned, axis=0), picks)
    return picks


def block_lane(planes, b, plane, core):
    source = lax.rem(plane - b // 2 + planes, planes)
    other = 1 - core if b % 2 else core
    return pl.multiple_of((2 * source + other) * ROWS, ROWS)


def program_terms(planes, exp_first, pick_first, exp_rest, pick_rest, trace_ref, _, mark_ref, own_ref, *out_refs):
    def mine(first, rest):
        tiles = [first[:, 0:ROWS]] + [
            rest[:, 2 * k * ROWS : (2 * k + 1) * ROWS] for k in range(planes - 1)
        ]
        return jnp.transpose(jnp.concatenate(tiles, axis=1))

    exps, picks = mine(exp_first, exp_rest), mine(pick_first, pick_rest)
    lanes = lax.broadcasted_iota(jnp.int32, (planes * ROWS, ROWS), 1).astype(F32) + 1.0
    values = [
        jnp.where(lanes == picks[:, q : q + 1], exps[:, q : q + 1], 0.0).astype(LOW)
        for q in range(8)
    ]
    total = dot(jnp.concatenate(values, axis=1), trace_ref[...])
    mark_ref[...] = total[0:8, 0:ROWS]
    own_ref[...] = total[0:ROWS, :]
    for k, out_ref in enumerate(out_refs, 1):
        out_ref[...] = total[k * ROWS : (k + 1) * ROWS, :].astype(LOW)


def trace_terms(planes, *refs):
    firsts, rests, sums, refs = refs[:4], refs[4:8], refs[8 : 8 + planes], refs[9 + planes :]
    total_ref, own_ref, x_ref, y_ref, xy_ref, high_ref, low_ref = refs
    plane, core = own_plane(), own_core()
    below = lax.broadcasted_iota(jnp.int32, (ROWS, ROWS), 0).astype(F32) + 1.0
    for b in range(2 * planes):
        exp_ref, pick_ref, pos_ref, _ = firsts if b < 2 else rests
        at = (b if b < 2 else b - 2) * ROWS
        lane = block_lane(planes, b, plane, core)
        total = jnp.exp(pos_ref[:, at : at + ROWS])
        for one in sums:
            total = total + one[:, pl.ds(lane, ROWS)]
        if b == 0:
            total_ref[...] = total
        scale = SCALE / total
        for i in range(4):
            q = 2 * i
            weight = exp_ref[q : q + 1, at : at + ROWS] * scale
            pick = pick_ref[q : q + 1, at : at + ROWS]
            high, low = halves(jnp.where(below == pick, weight, 0.0))
            high_ref[i * ROWS : (i + 1) * ROWS, b * ROWS : (b + 1) * ROWS] = high
            low_ref[i * ROWS : (i + 1) * ROWS, b * ROWS : (b + 1) * ROWS] = low
    first, rest = firsts[3][...], rests[3][...]
    edge = 2 * ROWS
    result = (
        dot(high_ref[:, 0:edge], first) + dot(low_ref[:, 0:edge], first)
        + dot(high_ref[:, edge:], rest) + dot(low_ref[:, edge:], rest)
    )
    own_ref[...] = result[0:ROWS, :]
    for i, out_ref in enumerate((x_ref, y_ref, xy_ref), 1):
        out_ref[...] = result[i * ROWS : (i + 1) * ROWS, :].astype(LOW)


def group_terms(*refs):
    highs, groups, (programs, traces, total_ref, trace_own) = refs[:4], refs[4:8], refs[8:12]
    prog_base, trace_base, prog_out, trace_out, size_ref, loss_ref = refs[12:]

    def joined(parts):
        return jnp.concatenate(parts, axis=0)

    trace = (joined([h[...] for h in highs]), joined([g[0:ROWS, :] for g in groups]))
    prog = (
        joined([g[ROWS : 2 * ROWS, :] for g in groups]),
        joined([g[2 * ROWS :, :] for g in groups]),
    )
    scores = SCALE * dot3(prog, trace, (1, 1))
    exps = jnp.exp(scores)
    total = jnp.sum(exps, axis=1, keepdims=True)
    weights = exps / total
    prog_unit, prog_len = normalize(programs[...])
    trace_unit, trace_len = normalize(traces[...])
    prog_out[...] = prog_unit
    trace_out[...] = trace_unit
    pos = SCALE * jnp.sum(prog_unit * trace_unit, axis=-1, keepdims=True)
    hard_total = to_column(total_ref[...])
    pull = jnp.exp(pos) / hard_total - 2.0
    lane = lax.broadcasted_iota(jnp.int32, (ROWS, ROWS), 1)
    sizes = jnp.where(lane == 0, prog_len, jnp.where(lane == 1, trace_len, SCALE / hard_total))
    size_ref[...] = sizes
    group_prog = dot3(halves(weights[0:ROWS, :]), trace)
    prog_base[...] = SCALE * (group_prog + pull * trace_unit)
    group_trace = dot3(halves(jnp.transpose(weights[:, 0:ROWS])), prog)
    trace_base[...] = SCALE * (group_trace + pull * prog_unit) + trace_own[...]
    loss_ref[...] = to_row(jnp.log(total[0:ROWS, :]) - 2.0 * pos) + jnp.log(total_ref[...])


def finish(planes, prog_base, trace_base, prog_unit, trace_unit, size_ref, *refs):
    progs, traces, (prog_out, trace_out) = refs[:planes], refs[planes : planes + 3], refs[planes + 3 :]
    back = trace_base[...]
    for one in traces:
        back = back + one[...].astype(F32)
    hard = progs[0][...]
    for one in progs[1:]:
        hard = hard + one[...].astype(F32)
    direction = prog_base[...] + size_ref[:, 2:3] * hard
    for unit, towards, length, out in (
        (prog_unit[...], direction, size_ref[:, 0:1], prog_out),
        (trace_unit[...], back, size_ref[:, 1:2], trace_out),
    ):
        along = jnp.sum(unit * towards, axis=-1, keepdims=True)
        out[...] = (towards - unit * along) / length


def call(body, outs, flops, moved, scratch=(), in_specs=None, limit=VMEM_LIMIT):
    return pl.pallas_call(
        body,
        out_shape=[jax.ShapeDtypeStruct(shape, dtype) for shape, dtype in outs],
        scratch_shapes=list(scratch),
        **({"in_specs": in_specs} if in_specs else {}),
        compiler_params=pltpu.CompilerParams(vmem_limit_bytes=limit),
        cost_estimate=pl.CostEstimate(flops=flops, bytes_accessed=moved, transcendentals=0),
    )


def passed_on(count, *refs):
    for source, target in zip(refs[:count], refs[-count:]):
        target[...] = source[...]


def after(values, *earlier):
    return call(
        functools.partial(passed_on, len(values)),
        [(value.shape, value.dtype) for value in values],
        0,
        0,
    )(*values, *earlier)


def on_device(dp_count, blk_count, programs, traces, hard_owner, hard_row):
    rows, feat = programs.shape
    planes = dp_count // 2
    size = dp_count * blk_count
    both = ("dp", "blk")

    def flipped(value, bits):
        return lax.ppermute(value, both, [(i, i ^ bits) for i in range(size)])

    def shifted(value, by):
        plane_size = 2 * blk_count
        return lax.ppermute(
            value, both, [(i, (i + by * plane_size) % size) for i in range(size)]
        )

    x_bit, y_bit = 2, blk_count
    block = rows * feat
    shape, width = (rows, feat), 2 * rows
    rest = (2 * planes - 2) * rows
    hbm = pl.BlockSpec(memory_space=pltpu.HBM)
    vmem = pl.BlockSpec(memory_space=pltpu.VMEM)
    index = hard_owner.shape[::-1]
    *msgs, high, group = call(
        functools.partial(prepare, planes),
        [((rows + 8, feat), LOW)] * planes + [(shape, LOW), ((3 * rows, feat), LOW)],
        10 * block,
        20 * block,
        [
            pltpu.VMEM(shape, F32),
            pltpu.VMEM(shape, F32),
            pltpu.VMEM(index, jnp.int32),
            pltpu.VMEM(index, jnp.int32),
            pltpu.VMEM((8 * planes, rows), F32),
            pltpu.SemaphoreType.DMA((4,)),
        ],
        [hbm] * 4,
        None,
    )(programs, traces, hard_owner.T, hard_row.T)
    own_msg = msgs[0]
    other_msg = flipped(own_msg, 1)
    high = after([high], other_msg)[0]
    *msgs, group = after([shifted(msgs[k], k) for k in range(1, planes)] + [group])
    group_x = flipped(group, x_bit)
    msgs = [one for msg in msgs for one in (msg, flipped(msg, 1))]
    highs = [high, flipped(high, x_bit), flipped(high, y_bit), flipped(high, x_bit + y_bit)]
    slots = [one for high in highs for one in (high, flipped(high, 1))]

    def lists(width):
        return [((8, width), F32), ((8, width), F32), ((1, width), F32), ((width, feat), LOW)]

    *first, sum_first, trace_all = call(
        score_first,
        lists(width) + [((1, width), F32), ((8 * rows, feat), LOW)],
        16 * rows * width * feat,
        8 * width * feat,
    )(own_msg, other_msg, *slots)
    *others, sums = call(
        functools.partial(score_rest, planes),
        lists(rest) + [((1, width + rest), F32)],
        16 * rows * rest * feat,
        4 * rest * feat,
    )(sum_first, trace_all, *msgs)
    all_sums = [sums] + [shifted(sums, k) for k in range(1, planes)]

    mark, prog_own, *prog_parts = call(
        functools.partial(program_terms, planes),
        [((8, rows), F32), (shape, F32)] + [(shape, LOW)] * (planes - 1),
        16 * rows * planes * rows * feat,
        4 * width * feat,
        (),
        [vmem] * 5 + [vmem],
    )(*first[:2], *others[:2], trace_all, flipped(sums, 1))
    prog_back = [shifted(part, -k) for k, part in enumerate(prog_parts, 1)]

    total, trace_own, part_x, part_y, part_xy = call(
        functools.partial(trace_terms, planes),
        [((1, rows), F32), (shape, F32)] + [(shape, LOW)] * 3,
        16 * rows * (width + rest) * feat,
        4 * width * feat,
        [pltpu.VMEM((4 * rows, width + rest), LOW)] * 2,
        [vmem] * (8 + planes) + [vmem],
    )(*first, *others, *all_sums, flipped(mark, 1))
    trace_back = [
        flipped(part_x, x_bit),
        flipped(part_y, y_bit),
        flipped(part_xy, x_bit + y_bit),
    ]

    group_x = after([group_x], total)[0]
    groups = [group, flipped(group, 1), group_x, flipped(group_x, 1)]
    *bases, loss = call(
        group_terms,
        [(shape, F32)] * 4 + [((rows, rows), F32), ((1, rows), F32)],
        block,
        block,
    )(*slots[:4], *groups, programs, traces, total, trace_own)

    grad_programs, grad_traces = call(
        functools.partial(finish, planes), [(shape, F32)] * 2, block, block
    )(*bases, prog_own, *prog_back, *trace_back)
    return grad_programs, grad_traces, loss.reshape(rows)


def solution(mesh):
    spec = P(("dp", "blk"), None)
    return jax.shard_map(
        functools.partial(on_device, mesh.shape["dp"], mesh.shape["blk"]),
        mesh=mesh,
        in_specs=(spec,) * 4,
        out_specs=(spec, spec, P(("dp", "blk"))),
        check_vma=False,
    )
```

```python
import functools

import jax
import jax.numpy as jnp
from jax import lax
from jax.experimental import pallas as pl
from jax.experimental.pallas import tpu as pltpu
from jax.sharding import PartitionSpec as P

EPSILON = 1e-06
SCALE = 14.0
LOW = jnp.bfloat16
F32 = jnp.float32
ROWS = 128
AHEAD = 2 * 10**9
VMEM_LIMIT = 40 * 1024 * 1024


def normalize(values):
    length = jnp.sqrt(jnp.sum(values * values, axis=-1, keepdims=True) + EPSILON)
    return values / length, length


def dot(a, b, contract=(1, 0)):
    return lax.dot_general(
        a, b, (((contract[0],), (contract[1],)), ((), ())), preferred_element_type=F32
    )


def halves(values):
    high = values.astype(LOW)
    return high, (values - high.astype(F32)).astype(LOW)


def dot3(a, b, contract=(1, 0)):
    return (
        dot(a[0], b[1], contract) + dot(a[1], b[0], contract)
    ) + dot(a[0], b[0], contract)


def eye():
    shape = (ROWS, ROWS)
    return lax.broadcasted_iota(jnp.int32, shape, 0) == lax.broadcasted_iota(jnp.int32, shape, 1)


def to_row(column):
    return jnp.sum(jnp.where(eye(), column, 0.0), axis=0, keepdims=True)


def to_column(row):
    return jnp.sum(jnp.where(eye(), row, 0.0), axis=1, keepdims=True)


def own_plane(planes):
    return lax.rem(lax.axis_index("dp"), planes)


def own_core():
    return lax.rem(lax.axis_index("blk"), 2)


def prepare(planes, *refs):
    sources, msg_refs, refs = refs[:4], refs[4 : 4 + planes], refs[4 + planes :]
    high_ref, buffers, pick_ref, sems = refs[0], refs[1:5], refs[5], refs[6]
    copies = [
        pltpu.make_async_copy(source, buffer, sems.at[i])
        for i, (source, buffer) in enumerate(zip(sources, buffers))
    ]
    for copy in copies:
        copy.start()
    for copy in copies:
        copy.wait()
    prog_ref, trace_ref, owner_ref, row_ref = buffers
    feat = prog_ref.shape[1]
    neg = owner_ref.shape[0]
    prog_unit, _ = normalize(prog_ref[...])
    trace_unit, _ = normalize(trace_ref[...])
    prog_high = prog_unit.astype(LOW)
    high_ref[...] = trace_unit.astype(LOW)
    pos = to_row(SCALE * jnp.sum(prog_unit * trace_unit, axis=-1, keepdims=True))
    high = pos.astype(LOW).astype(F32)
    mid = (pos - high).astype(LOW).astype(F32)
    last = pos - high - mid
    line = lax.broadcasted_iota(jnp.int32, (8, ROWS), 0)
    pos_tile = jnp.where(line == 0, high, jnp.where(line == 1, mid, jnp.where(line == 2, last, 0.0)))
    owners = owner_ref[...]
    rows = row_ref[...].astype(F32) + 1.0
    line = lax.broadcasted_iota(jnp.int32, (planes * 8, ROWS), 0)
    index = (lax.shift_right_logical(line, 2) & 1) * (4 * planes) + lax.shift_right_logical(line, 3) * 4 + (line & 3)
    picks = jnp.zeros((planes * 8, ROWS), F32)
    for n in range(neg):
        picks = picks + jnp.where(index == owners[n : n + 1, :], rows[n : n + 1, :], 0.0)
    pick_ref[...] = picks
    plane = own_plane(planes)
    rest = jnp.zeros((8, feat - 2 * ROWS), F32)
    for k, msg_ref in enumerate(msg_refs):
        at = pl.multiple_of(8 * (plane ^ k), 8)
        aux = jnp.concatenate([pick_ref[pl.ds(at, 8), :], pos_tile, rest], axis=1)
        msg_ref[0:ROWS, :] = prog_high
        msg_ref[ROWS:, :] = aux.astype(LOW)


def group_parts(prog_ref, trace_ref, *refs):
    _, refs[-1][0:ROWS, :] = halves(normalize(trace_ref[...])[0])
    refs[-1][ROWS : 2 * ROWS, :], refs[-1][2 * ROWS :, :] = halves(normalize(prog_ref[...])[0])


def score_block(planes, msgs, trace_ref, exp_ref, pick_ref, pos_ref, prog_ref):
    for b, msg in enumerate(msgs):
        lanes = slice(b * ROWS, (b + 1) * ROWS)
        prog_ref[lanes, :] = msg[0:ROWS, :]
        aux = msg[ROWS:, :].astype(F32)
        pick_ref[:, lanes] = by_slot(planes, aux[:, 0:ROWS])
        pos = aux[:, ROWS : 2 * ROWS]
        pos_ref[:, lanes] = pos[0:1, :] + pos[1:2, :] + pos[2:3, :]
    width = len(msgs) * ROWS
    below = lax.broadcasted_iota(jnp.int32, (ROWS, width), 0).astype(F32) + 1.0
    sums = jnp.zeros((1, width), F32)
    all_scores = dot(trace_ref[...], prog_ref[...], (1, 1))
    for q in range(8):
        scores = all_scores[q * ROWS : (q + 1) * ROWS, :]
        pick = pick_ref[q : q + 1, :]
        found = jnp.sum(jnp.where(below == pick, scores, 0.0), axis=0, keepdims=True)
        exps = jnp.where(pick > 0.0, jnp.exp(SCALE * found), 0.0)
        exp_ref[q : q + 1, :] = exps
        sums = sums + exps
    return sums


def score_first(planes, own_ref, other_ref, *refs):
    traces, (exp_ref, pick_ref, pos_ref, prog_ref, sum_ref, trace_ref) = refs[:8], refs[8:]
    for q in range(8):
        trace_ref[q * ROWS : (q + 1) * ROWS, :] = traces[q][...]
    sum_ref[...] = score_block(
        planes, (own_ref, other_ref), trace_ref, exp_ref, pick_ref, pos_ref, prog_ref
    )


def score_rest(planes, sum_in, trace_ref, *refs):
    count = 2 * planes - 2
    msgs, (exp_ref, pick_ref, pos_ref, prog_ref, sum_ref) = refs[:count], refs[count:]
    sums = score_block(planes, msgs, trace_ref, exp_ref, pick_ref, pos_ref, prog_ref)
    plane, core = own_plane(planes), own_core()
    for b in range(count + 2):
        part = sum_in[:, b * ROWS : (b + 1) * ROWS] if b < 2 else sums[:, (b - 2) * ROWS : (b - 1) * ROWS]
        sum_ref[:, pl.ds(block_lane(b, plane, core), ROWS)] = part


def by_slot(planes, picks):
    blk = lax.axis_index("blk")
    bits = (lax.rem(blk, 2), lax.div(blk, 2), lax.div(lax.axis_index("dp"), planes))
    for step, bit in zip((1, 2, 4), bits):
        turned = []
        for at in range(0, 8, 2 * step):
            turned += [picks[at + step : at + 2 * step, :], picks[at : at + step, :]]
        picks = jnp.where(bit == 1, jnp.concatenate(turned, axis=0), picks)
    return picks


def block_lane(b, plane, core):
    return pl.multiple_of((2 * (plane ^ (b // 2)) + (core ^ (b % 2))) * ROWS, ROWS)


def program_terms(planes, exp_first, pick_first, exp_rest, pick_rest, trace_ref, _, mark_ref, own_ref, *out_refs):
    def mine(first, rest):
        tiles = [first[:, 0:ROWS]] + [
            rest[:, 2 * k * ROWS : (2 * k + 1) * ROWS] for k in range(planes - 1)
        ]
        return jnp.transpose(jnp.concatenate(tiles, axis=1))

    exps, picks = mine(exp_first, exp_rest), mine(pick_first, pick_rest)
    lanes = lax.broadcasted_iota(jnp.int32, (planes * ROWS, ROWS), 1).astype(F32) + 1.0
    values = [
        jnp.where(lanes == picks[:, q : q + 1], exps[:, q : q + 1], 0.0).astype(LOW)
        for q in range(8)
    ]
    total = dot(jnp.concatenate(values, axis=1), trace_ref[...])
    mark_ref[...] = total[0:8, 0:ROWS]
    own_ref[...] = total[0:ROWS, :]
    for k, out_ref in enumerate(out_refs, 1):
        out_ref[...] = total[k * ROWS : (k + 1) * ROWS, :].astype(LOW)


def trace_terms(planes, *refs):
    firsts, rests, sums, refs = refs[:4], refs[4:8], refs[8 : 8 + planes], refs[9 + planes :]
    total_ref, own_ref, x_ref, h_ref, xh_ref, high_ref, low_ref = refs
    plane, core = own_plane(planes), own_core()
    below = lax.broadcasted_iota(jnp.int32, (ROWS, ROWS), 0).astype(F32) + 1.0
    for b in range(2 * planes):
        exp_ref, pick_ref, pos_ref, _ = firsts if b < 2 else rests
        at = (b if b < 2 else b - 2) * ROWS
        lane = block_lane(b, plane, core)
        total = jnp.exp(pos_ref[:, at : at + ROWS])
        for one in sums:
            total = total + one[:, pl.ds(lane, ROWS)]
        if b == 0:
            total_ref[...] = total
        scale = SCALE / total
        for i in range(4):
            q = 2 * i
            weight = exp_ref[q : q + 1, at : at + ROWS] * scale
            pick = pick_ref[q : q + 1, at : at + ROWS]
            high, low = halves(jnp.where(below == pick, weight, 0.0))
            high_ref[i * ROWS : (i + 1) * ROWS, b * ROWS : (b + 1) * ROWS] = high
            low_ref[i * ROWS : (i + 1) * ROWS, b * ROWS : (b + 1) * ROWS] = low
    first, rest = firsts[3][...], rests[3][...]
    edge = 2 * ROWS
    result = (
        dot(high_ref[:, 0:edge], first) + dot(low_ref[:, 0:edge], first)
        + dot(high_ref[:, edge:], rest) + dot(low_ref[:, edge:], rest)
    )
    own_ref[...] = result[0:ROWS, :]
    for i, out_ref in enumerate((x_ref, h_ref, xh_ref), 1):
        out_ref[...] = result[i * ROWS : (i + 1) * ROWS, :].astype(out_ref.dtype)


def added(own_ref, other_ref, x_ref, out_ref, x_out):
    out_ref[...] = (own_ref[...] + other_ref[...].astype(F32)).astype(LOW)
    x_out[...] = x_ref[...]


def group_terms(*refs):
    highs, groups, (programs, traces, total_ref, trace_own) = refs[:4], refs[4:6], refs[6:10]
    prog_base, trace_base, prog_out, trace_out, size_ref, loss_ref = refs[10:]

    def part(which):
        at = [(x * 3 + which) * ROWS for x in range(2)]
        return jnp.concatenate([g[a : a + ROWS, :] for a in at for g in groups], axis=0)

    trace = (jnp.concatenate([h[...] for h in highs], axis=0), part(0))
    prog = (part(1), part(2))
    scores = SCALE * dot3(prog, trace, (1, 1))
    exps = jnp.exp(scores)
    total = jnp.sum(exps, axis=1, keepdims=True)
    weights = exps / total
    prog_unit, prog_len = normalize(programs[...])
    trace_unit, trace_len = normalize(traces[...])
    prog_out[...] = prog_unit
    trace_out[...] = trace_unit
    pos = SCALE * jnp.sum(prog_unit * trace_unit, axis=-1, keepdims=True)
    hard_total = to_column(total_ref[...])
    pull = jnp.exp(pos) / hard_total - 2.0
    lane = lax.broadcasted_iota(jnp.int32, (ROWS, ROWS), 1)
    sizes = jnp.where(lane == 0, prog_len, jnp.where(lane == 1, trace_len, SCALE / hard_total))
    size_ref[...] = sizes
    group_prog = dot3(halves(weights[0:ROWS, :]), trace)
    prog_base[...] = SCALE * (group_prog + pull * trace_unit)
    group_trace = dot3(halves(jnp.transpose(weights[:, 0:ROWS])), prog)
    trace_base[...] = SCALE * (group_trace + pull * prog_unit) + trace_own[...]
    loss_ref[...] = to_row(jnp.log(total[0:ROWS, :]) - 2.0 * pos) + jnp.log(total_ref[...])


def finish(planes, prog_base, trace_base, prog_unit, trace_unit, size_ref, *refs):
    progs, traces, (prog_out, trace_out) = refs[:planes], refs[planes : planes + 2], refs[planes + 2 :]
    back = trace_base[...]
    for one in traces:
        back = back + one[...].astype(F32)
    hard = progs[0][...]
    for one in progs[1:]:
        hard = hard + one[...].astype(F32)
    direction = prog_base[...] + size_ref[:, 2:3] * hard
    for unit, towards, length, out in (
        (prog_unit[...], direction, size_ref[:, 0:1], prog_out),
        (trace_unit[...], back, size_ref[:, 1:2], trace_out),
    ):
        along = jnp.sum(unit * towards, axis=-1, keepdims=True)
        out[...] = (towards - unit * along) / length


def call(body, outs, flops, moved, scratch=(), in_specs=None, limit=VMEM_LIMIT):
    return pl.pallas_call(
        body,
        out_shape=[jax.ShapeDtypeStruct(shape, dtype) for shape, dtype in outs],
        scratch_shapes=list(scratch),
        **({"in_specs": in_specs} if in_specs else {}),
        compiler_params=pltpu.CompilerParams(vmem_limit_bytes=limit),
        cost_estimate=pl.CostEstimate(flops=flops, bytes_accessed=moved, transcendentals=0),
    )


def joined(own_ref, x_ref, _, out_ref):
    out_ref[0 : 3 * ROWS, :] = own_ref[...]
    out_ref[3 * ROWS :, :] = x_ref[...]


def passed_on(count, *refs):
    for source, target in zip(refs[:count], refs[-count:]):
        target[...] = source[...]


def after(values, *earlier, cost=0):
    return call(
        functools.partial(passed_on, len(values)),
        [(value.shape, value.dtype) for value in values],
        cost,
        0,
    )(*values, *earlier)


def on_device(dp_count, blk_count, programs, traces, hard_owner, hard_row):
    rows, feat = programs.shape
    planes = dp_count // 2
    size = dp_count * blk_count
    both = ("dp", "blk")

    def flipped(value, bits):
        return lax.ppermute(value, both, [(i, i ^ bits) for i in range(size)])

    def to_plane(value, k):
        return flipped(value, k * blk_count)

    x_bit, h_bit = 2, planes * blk_count
    block = rows * feat
    shape, width = (rows, feat), 2 * rows
    rest = (2 * planes - 2) * rows
    hbm = pl.BlockSpec(memory_space=pltpu.HBM)
    vmem = pl.BlockSpec(memory_space=pltpu.VMEM)
    index = hard_owner.shape[::-1]
    *sent, high = call(
        functools.partial(prepare, planes),
        [((rows + 8, feat), LOW)] * planes + [(shape, LOW)],
        10 * block,
        20 * block,
        [
            pltpu.VMEM(shape, F32),
            pltpu.VMEM(shape, F32),
            pltpu.VMEM(index, jnp.int32),
            pltpu.VMEM(index, jnp.int32),
            pltpu.VMEM((8 * planes, rows), F32),
            pltpu.SemaphoreType.DMA((4,)),
        ],
        [hbm] * 4,
        None,
    )(programs, traces, hard_owner.T, hard_row.T)
    far_first = list(range(planes - 1, 0, -1))
    high_h = flipped(high, h_bit)
    msgs = [sent[0], *after([to_plane(sent[k], k) for k in far_first], cost=AHEAD)[::-1]]
    highs = [high, flipped(high, x_bit), high_h, flipped(high_h, x_bit)]
    group = call(group_parts, [((3 * rows, feat), LOW)], 10 * block, 20 * block)(
        programs, traces, high_h
    )[0]
    msgs = [one for k in range(planes) for one in (msgs[k], flipped(msgs[k], 1))]
    slots = [one for high in highs for one in (high, flipped(high, 1))]
    group_x = flipped(group, x_bit)

    def lists(width):
        return [((8, width), F32), ((8, width), F32), ((1, width), F32), ((width, feat), LOW)]

    *first, sum_first, trace_all = call(
        functools.partial(score_first, planes),
        lists(width) + [((1, width), F32), ((8 * rows, feat), LOW)],
        16 * rows * width * feat,
        8 * width * feat,
    )(*msgs[:2], *slots)
    *others, sums = call(
        functools.partial(score_rest, planes),
        lists(rest) + [((1, width + rest), F32)],
        16 * rows * rest * feat,
        4 * rest * feat,
    )(sum_first, trace_all, *msgs[2:])
    all_sums = [sums] + [to_plane(sums, k) for k in far_first]

    mark, prog_own, *prog_parts = call(
        functools.partial(program_terms, planes),
        [((8, rows), F32), (shape, F32)] + [(shape, LOW)] * (planes - 1),
        16 * rows * planes * rows * feat,
        4 * width * feat,
        (),
        [vmem] * 5 + [vmem],
    )(*first[:2], *others[:2], trace_all, flipped(sums, 1))
    total, trace_own, part_x, part_h, part_xh = call(
        functools.partial(trace_terms, planes),
        [((1, rows), F32), (shape, F32), (shape, LOW), (shape, F32), (shape, LOW)],
        16 * rows * (width + rest) * feat,
        4 * width * feat,
        [pltpu.VMEM((4 * rows, width + rest), LOW)] * 2,
        [vmem] * (8 + planes) + [vmem],
    )(*first, *others, *all_sums, flipped(mark, 1))
    for_h, part_x = call(added, [(shape, LOW)] * 2, block, 4 * block)(
        part_h, flipped(part_xh, x_bit), part_x
    )
    trace_back = [flipped(for_h, h_bit), flipped(part_x, x_bit)]

    groups = call(joined, [((6 * rows, feat), LOW)], 0, 0)(group, group_x, total)[0]
    prog_back = [to_plane(part, k) for k, part in enumerate(prog_parts, 1)]
    *bases, loss = call(
        group_terms,
        [(shape, F32)] * 4 + [((rows, rows), F32), ((1, rows), F32)],
        block,
        block,
    )(*slots[:4], groups, flipped(groups, 1), programs, traces, total, trace_own)

    grad_programs, grad_traces = call(
        functools.partial(finish, planes), [(shape, F32)] * 2, block, block
    )(*bases, prog_own, *prog_back, *trace_back)
    return grad_programs, grad_traces, loss.reshape(rows)


def solution(mesh):
    spec = P(("dp", "blk"), None)
    return jax.shard_map(
        functools.partial(on_device, mesh.shape["dp"], mesh.shape["blk"]),
        mesh=mesh,
        in_specs=(spec,) * 4,
        out_specs=(spec, spec, P(("dp", "blk"))),
        check_vma=False,
    )
```

```python
import functools

import jax
import jax.numpy as jnp
from jax import lax
from jax.experimental import pallas as pl
from jax.experimental.pallas import tpu as pltpu
from jax.sharding import PartitionSpec as P

EPSILON = 1e-06
SCALE = 14.0
LOW = jnp.bfloat16
F32 = jnp.float32
ROWS = 128
AHEAD = 2 * 10**9
JOIN = 0
VMEM_LIMIT = 40 * 1024 * 1024


def normalize(values):
    length = jnp.sqrt(jnp.sum(values * values, axis=-1, keepdims=True) + EPSILON)
    return values / length, length


def dot(a, b, contract=(1, 0)):
    return lax.dot_general(
        a, b, (((contract[0],), (contract[1],)), ((), ())), preferred_element_type=F32
    )


def halves(values):
    high = values.astype(LOW)
    return high, (values - high.astype(F32)).astype(LOW)


def dot3(a, b, contract=(1, 0)):
    return (
        dot(a[0], b[1], contract) + dot(a[1], b[0], contract)
    ) + dot(a[0], b[0], contract)


def eye():
    shape = (ROWS, ROWS)
    return lax.broadcasted_iota(jnp.int32, shape, 0) == lax.broadcasted_iota(jnp.int32, shape, 1)


def to_row(column):
    return jnp.sum(jnp.where(eye(), column, 0.0), axis=0, keepdims=True)


def to_column(row):
    return jnp.sum(jnp.where(eye(), row, 0.0), axis=1, keepdims=True)


def own_plane(planes):
    return lax.rem(lax.axis_index("dp"), planes)


def own_core():
    return lax.rem(lax.axis_index("blk"), 2)


def prepare(planes, *refs):
    sources, msg_refs, refs = refs[:4], refs[4 : 4 + planes], refs[4 + planes :]
    high_ref, buffers, pick_ref, sems = refs[0], refs[1:5], refs[5], refs[6]
    copies = [
        pltpu.make_async_copy(source, buffer, sems.at[i])
        for i, (source, buffer) in enumerate(zip(sources, buffers))
    ]
    for copy in copies:
        copy.start()
    for copy in copies:
        copy.wait()
    prog_ref, trace_ref, owner_ref, row_ref = buffers
    feat = prog_ref.shape[1]
    neg = owner_ref.shape[0]
    prog_unit, _ = normalize(prog_ref[...])
    trace_unit, _ = normalize(trace_ref[...])
    prog_high = prog_unit.astype(LOW)
    high_ref[...] = trace_unit.astype(LOW)
    pos = to_row(SCALE * jnp.sum(prog_unit * trace_unit, axis=-1, keepdims=True))
    high = pos.astype(LOW).astype(F32)
    mid = (pos - high).astype(LOW).astype(F32)
    last = pos - high - mid
    line = lax.broadcasted_iota(jnp.int32, (8, ROWS), 0)
    pos_tile = jnp.where(line == 0, high, jnp.where(line == 1, mid, jnp.where(line == 2, last, 0.0)))
    owners = owner_ref[...]
    rows = row_ref[...].astype(F32) + 1.0
    line = lax.broadcasted_iota(jnp.int32, (planes * 8, ROWS), 0)
    index = (lax.shift_right_logical(line, 2) & 1) * (4 * planes) + lax.shift_right_logical(line, 3) * 4 + (line & 3)
    picks = jnp.zeros((planes * 8, ROWS), F32)
    for n in range(neg):
        picks = picks + jnp.where(index == owners[n : n + 1, :], rows[n : n + 1, :], 0.0)
    pick_ref[...] = picks
    plane = own_plane(planes)
    rest = jnp.zeros((8, feat - 2 * ROWS), F32)
    for k, msg_ref in enumerate(msg_refs):
        at = pl.multiple_of(8 * (plane ^ k), 8)
        aux = jnp.concatenate([pick_ref[pl.ds(at, 8), :], pos_tile, rest], axis=1)
        msg_ref[0:ROWS, :] = prog_high
        msg_ref[ROWS:, :] = aux.astype(LOW)


def group_parts(prog_ref, trace_ref, *refs):
    _, refs[-1][0:ROWS, :] = halves(normalize(trace_ref[...])[0])
    refs[-1][ROWS : 2 * ROWS, :], refs[-1][2 * ROWS :, :] = halves(normalize(prog_ref[...])[0])


def score_block(planes, msgs, trace_ref, exp_ref, pick_ref, pos_ref, prog_ref):
    for b, msg in enumerate(msgs):
        lanes = slice(b * ROWS, (b + 1) * ROWS)
        prog_ref[lanes, :] = msg[0:ROWS, :]
        aux = msg[ROWS:, :].astype(F32)
        pick_ref[:, lanes] = by_slot(planes, aux[:, 0:ROWS])
        pos = aux[:, ROWS : 2 * ROWS]
        pos_ref[:, lanes] = pos[0:1, :] + pos[1:2, :] + pos[2:3, :]
    width = len(msgs) * ROWS
    below = lax.broadcasted_iota(jnp.int32, (ROWS, width), 0).astype(F32) + 1.0
    sums = jnp.zeros((1, width), F32)
    all_scores = dot(trace_ref[...], prog_ref[...], (1, 1))
    for q in range(8):
        scores = all_scores[q * ROWS : (q + 1) * ROWS, :]
        pick = pick_ref[q : q + 1, :]
        found = jnp.sum(jnp.where(below == pick, scores, 0.0), axis=0, keepdims=True)
        exps = jnp.where(pick > 0.0, jnp.exp(SCALE * found), 0.0)
        exp_ref[q : q + 1, :] = exps
        sums = sums + exps
    return sums


def score_first(planes, own_ref, other_ref, *refs):
    traces, (exp_ref, pick_ref, pos_ref, prog_ref, sum_ref, trace_ref) = refs[:8], refs[8:]
    for q in range(8):
        trace_ref[q * ROWS : (q + 1) * ROWS, :] = traces[q][...]
    sum_ref[...] = score_block(
        planes, (own_ref, other_ref), trace_ref, exp_ref, pick_ref, pos_ref, prog_ref
    )


def score_rest(planes, sum_in, trace_ref, *refs):
    count = 2 * planes - 2
    msgs, (exp_ref, pick_ref, pos_ref, prog_ref, sum_ref) = refs[:count], refs[count:]
    sums = score_block(planes, msgs, trace_ref, exp_ref, pick_ref, pos_ref, prog_ref)
    plane, core = own_plane(planes), own_core()
    for b in range(count + 2):
        part = sum_in[:, b * ROWS : (b + 1) * ROWS] if b < 2 else sums[:, (b - 2) * ROWS : (b - 1) * ROWS]
        sum_ref[:, pl.ds(block_lane(b, plane, core), ROWS)] = part


def by_slot(planes, picks):
    blk = lax.axis_index("blk")
    bits = (lax.rem(blk, 2), lax.div(blk, 2), lax.div(lax.axis_index("dp"), planes))
    for step, bit in zip((1, 2, 4), bits):
        turned = []
        for at in range(0, 8, 2 * step):
            turned += [picks[at + step : at + 2 * step, :], picks[at : at + step, :]]
        picks = jnp.where(bit == 1, jnp.concatenate(turned, axis=0), picks)
    return picks


def block_lane(b, plane, core):
    return pl.multiple_of((2 * (plane ^ (b // 2)) + (core ^ (b % 2))) * ROWS, ROWS)


def program_terms(planes, exp_first, pick_first, exp_rest, pick_rest, trace_ref, _, mark_ref, own_ref, *out_refs):
    def mine(first, rest):
        tiles = [first[:, 0:ROWS]] + [
            rest[:, 2 * k * ROWS : (2 * k + 1) * ROWS] for k in range(planes - 1)
        ]
        return jnp.transpose(jnp.concatenate(tiles, axis=1))

    exps, picks = mine(exp_first, exp_rest), mine(pick_first, pick_rest)
    lanes = lax.broadcasted_iota(jnp.int32, (planes * ROWS, ROWS), 1).astype(F32) + 1.0
    values = [
        jnp.where(lanes == picks[:, q : q + 1], exps[:, q : q + 1], 0.0).astype(LOW)
        for q in range(8)
    ]
    total = dot(jnp.concatenate(values, axis=1), trace_ref[...])
    mark_ref[...] = total[0:8, 0:ROWS]
    own_ref[...] = total[0:ROWS, :]
    for k, out_ref in enumerate(out_refs, 1):
        out_ref[...] = total[k * ROWS : (k + 1) * ROWS, :].astype(LOW)


def far_terms(planes, *refs):
    firsts, rests, sums, refs = refs[:4], refs[4:8], refs[8 : 8 + planes], refs[9 + planes :]
    total_ref, weight_ref, far_ref = refs
    plane, core = own_plane(planes), own_core()
    for b in range(2 * planes):
        exp_ref, pick_ref, pos_ref, _ = firsts if b < 2 else rests
        at = (b if b < 2 else b - 2) * ROWS
        lane = block_lane(b, plane, core)
        total = jnp.exp(pos_ref[:, at : at + ROWS])
        for one in sums:
            total = total + one[:, pl.ds(lane, ROWS)]
        if b == 0:
            total_ref[...] = total
        weight_ref[:, b * ROWS : (b + 1) * ROWS] = exp_ref[:, at : at + ROWS] * (SCALE / total)
    picks = jnp.concatenate([firsts[1][...], rests[1][...]], axis=1)
    progs = firsts[3][...], rests[3][...]
    far_ref[...] = weighted(weight_ref[...], picks, progs, (6,)).astype(LOW)


def weighted(weights, picks, progs, slots):
    below = lax.broadcasted_iota(jnp.int32, (ROWS, weights.shape[1]), 0).astype(F32) + 1.0
    high = weights.astype(LOW).astype(F32)
    low = weights - high
    pairs = [[], []]
    for q in slots:
        chosen = below == picks[q : q + 1, :]
        for rows, part in zip(pairs, (high, low)):
            rows.append(jnp.where(chosen, part[q : q + 1, :], 0.0).astype(LOW))
    edge = progs[0].shape[0]
    result = 0.0
    for rows in pairs:
        values = jnp.concatenate(rows, axis=0)
        result = result + dot(values[:, :edge], progs[0]) + dot(values[:, edge:], progs[1])
    return result


def near_terms(weight_ref, pick_first, pick_rest, prog_first, prog_rest, own_ref, x_ref, h_ref):
    picks = jnp.concatenate([pick_first[...], pick_rest[...]], axis=1)
    result = weighted(weight_ref[...], picks, (prog_first[...], prog_rest[...]), (0, 2, 4))
    own_ref[...] = result[0:ROWS, :]
    x_ref[...] = result[ROWS : 2 * ROWS, :].astype(LOW)
    h_ref[...] = result[2 * ROWS :, :]


def added(own_ref, other_ref, x_ref, out_ref, x_out):
    out_ref[...] = (own_ref[...] + other_ref[...].astype(F32)).astype(LOW)
    x_out[...] = x_ref[...]


def group_terms(*refs):
    highs, groups, (programs, traces, total_ref, trace_own) = refs[:4], refs[4:6], refs[6:10]
    prog_base, trace_base, prog_out, trace_out, size_ref, loss_ref = refs[10:]

    def part(which):
        at = [(x * 3 + which) * ROWS for x in range(2)]
        return jnp.concatenate([g[a : a + ROWS, :] for a in at for g in groups], axis=0)

    trace = (jnp.concatenate([h[...] for h in highs], axis=0), part(0))
    prog = (part(1), part(2))
    scores = SCALE * dot3(prog, trace, (1, 1))
    exps = jnp.exp(scores)
    total = jnp.sum(exps, axis=1, keepdims=True)
    weights = exps / total
    prog_unit, prog_len = normalize(programs[...])
    trace_unit, trace_len = normalize(traces[...])
    prog_out[...] = prog_unit
    trace_out[...] = trace_unit
    pos = SCALE * jnp.sum(prog_unit * trace_unit, axis=-1, keepdims=True)
    hard_total = to_column(total_ref[...])
    pull = jnp.exp(pos) / hard_total - 2.0
    lane = lax.broadcasted_iota(jnp.int32, (ROWS, ROWS), 1)
    sizes = jnp.where(lane == 0, prog_len, jnp.where(lane == 1, trace_len, SCALE / hard_total))
    size_ref[...] = sizes
    group_prog = dot3(halves(weights[0:ROWS, :]), trace)
    prog_base[...] = SCALE * (group_prog + pull * trace_unit)
    group_trace = dot3(halves(jnp.transpose(weights[:, 0:ROWS])), prog)
    trace_base[...] = SCALE * (group_trace + pull * prog_unit) + trace_own[...]
    loss_ref[...] = to_row(jnp.log(total[0:ROWS, :]) - 2.0 * pos) + jnp.log(total_ref[...])


def finish(planes, prog_base, trace_base, prog_unit, trace_unit, size_ref, *refs):
    progs, traces, (prog_out, trace_out) = refs[:planes], refs[planes : planes + 2], refs[planes + 2 :]
    back = trace_base[...]
    for one in traces:
        back = back + one[...].astype(F32)
    hard = progs[0][...]
    for one in progs[1:]:
        hard = hard + one[...].astype(F32)
    direction = prog_base[...] + size_ref[:, 2:3] * hard
    for unit, towards, length, out in (
        (prog_unit[...], direction, size_ref[:, 0:1], prog_out),
        (trace_unit[...], back, size_ref[:, 1:2], trace_out),
    ):
        along = jnp.sum(unit * towards, axis=-1, keepdims=True)
        out[...] = (towards - unit * along) / length


def call(body, outs, flops, moved, scratch=(), in_specs=None, limit=VMEM_LIMIT):
    return pl.pallas_call(
        body,
        out_shape=[jax.ShapeDtypeStruct(shape, dtype) for shape, dtype in outs],
        scratch_shapes=list(scratch),
        **({"in_specs": in_specs} if in_specs else {}),
        compiler_params=pltpu.CompilerParams(vmem_limit_bytes=limit),
        cost_estimate=pl.CostEstimate(flops=flops, bytes_accessed=moved, transcendentals=0),
    )


def joined(own_ref, x_ref, _, out_ref):
    out_ref[0 : 3 * ROWS, :] = own_ref[...]
    out_ref[3 * ROWS :, :] = x_ref[...]


def passed_on(count, *refs):
    for source, target in zip(refs[:count], refs[-count:]):
        target[...] = source[...]


def after(values, *earlier, cost=0):
    return call(
        functools.partial(passed_on, len(values)),
        [(value.shape, value.dtype) for value in values],
        cost,
        0,
    )(*values, *earlier)


def on_device(dp_count, blk_count, programs, traces, hard_owner, hard_row):
    rows, feat = programs.shape
    planes = dp_count // 2
    size = dp_count * blk_count
    both = ("dp", "blk")

    def flipped(value, bits):
        return lax.ppermute(value, both, [(i, i ^ bits) for i in range(size)])

    def to_plane(value, k):
        return flipped(value, k * blk_count)

    x_bit, h_bit = 2, planes * blk_count
    block = rows * feat
    shape, width = (rows, feat), 2 * rows
    rest = (2 * planes - 2) * rows
    hbm = pl.BlockSpec(memory_space=pltpu.HBM)
    vmem = pl.BlockSpec(memory_space=pltpu.VMEM)
    index = hard_owner.shape[::-1]
    *sent, high = call(
        functools.partial(prepare, planes),
        [((rows + 8, feat), LOW)] * planes + [(shape, LOW)],
        10 * block,
        20 * block,
        [
            pltpu.VMEM(shape, F32),
            pltpu.VMEM(shape, F32),
            pltpu.VMEM(index, jnp.int32),
            pltpu.VMEM(index, jnp.int32),
            pltpu.VMEM((8 * planes, rows), F32),
            pltpu.SemaphoreType.DMA((4,)),
        ],
        [hbm] * 4,
        None,
    )(programs, traces, hard_owner.T, hard_row.T)
    far_first = list(range(planes - 1, 0, -1))
    high_h = flipped(high, h_bit)
    msgs = [sent[0], *after([to_plane(sent[k], k) for k in far_first], cost=AHEAD)[::-1]]
    highs = [high, flipped(high, x_bit), high_h, flipped(high_h, x_bit)]
    group = call(group_parts, [((3 * rows, feat), LOW)], 10 * block, 20 * block)(
        programs, traces, high_h
    )[0]
    msgs = [one for k in range(planes) for one in (msgs[k], flipped(msgs[k], 1))]
    slots = [one for high in highs for one in (high, flipped(high, 1))]
    group_x = flipped(group, x_bit)

    def lists(width):
        return [((8, width), F32), ((8, width), F32), ((1, width), F32), ((width, feat), LOW)]

    *first, sum_first, trace_all = call(
        functools.partial(score_first, planes),
        lists(width) + [((1, width), F32), ((8 * rows, feat), LOW)],
        10**8,
        0,
    )(*msgs[:2], *slots)
    *others, sums = call(
        functools.partial(score_rest, planes),
        lists(rest) + [((1, width + rest), F32)],
        3 * 10**8,
        0,
    )(sum_first, trace_all, *msgs[2:])
    all_sums = [sums] + [to_plane(sums, k) for k in far_first]

    mark, prog_own, *prog_parts = call(
        functools.partial(program_terms, planes),
        [((8, rows), F32), (shape, F32)] + [(shape, LOW)] * (planes - 1),
        AHEAD,
        4 * width * feat,
        (),
        [vmem] * 5 + [vmem],
    )(*first[:2], *others[:2], trace_all, sums)
    wide = (8, width + rest)
    total, weights, part_xh = call(
        functools.partial(far_terms, planes),
        [((1, rows), F32), (wide, F32), (shape, LOW)],
        0,
        0,
        (),
        [vmem] * (9 + planes),
    )(*first, *others, *all_sums, mark)
    trace_own, part_x, part_h = call(
        near_terms,
        [(shape, F32), (shape, LOW), (shape, F32)],
        12 * rows * (width + rest) * feat,
        4 * width * feat,
    )(weights, first[1], others[1], first[3], others[3])
    for_h, part_x = call(added, [(shape, LOW)] * 2, block, 4 * block)(
        part_h, flipped(part_xh, x_bit), part_x
    )
    trace_back = [flipped(for_h, h_bit), flipped(part_x, x_bit)]

    groups = call(joined, [((6 * rows, feat), LOW)], JOIN, 0)(group, group_x, total)[0]
    prog_back = [to_plane(part, k) for k, part in enumerate(prog_parts, 1)]
    *bases, loss = call(
        group_terms,
        [(shape, F32)] * 4 + [((rows, rows), F32), ((1, rows), F32)],
        block,
        block,
    )(*slots[:4], groups, flipped(groups, 1), programs, traces, total, trace_own)

    grad_programs, grad_traces = call(
        functools.partial(finish, planes), [(shape, F32)] * 2, block, block
    )(*bases, prog_own, *prog_back, *trace_back)
    return grad_programs, grad_traces, loss.reshape(rows)


def solution(mesh):
    spec = P(("dp", "blk"), None)
    return jax.shard_map(
        functools.partial(on_device, mesh.shape["dp"], mesh.shape["blk"]),
        mesh=mesh,
        in_specs=(spec,) * 4,
        out_specs=(spec, spec, P(("dp", "blk"))),
        check_vma=False,
    )
```

```python
import functools

import jax
import jax.numpy as jnp
from jax import lax
from jax.experimental import pallas as pl
from jax.experimental.pallas import tpu as pltpu
from jax.sharding import PartitionSpec as P

EPSILON = 1e-06
SCALE = 14.0
LOW = jnp.bfloat16
F32 = jnp.float32
ROWS = 128
AHEAD = 2 * 10**9
NEAR = 10**8
FAR = 5*10**9
HALF = 2*10**9
STACK = 0
TRACE = 4*10**9
LAST = 3*10**8
JOIN = 0
VMEM_LIMIT = 40 * 1024 * 1024


def normalize(values):
    length = jnp.sqrt(jnp.sum(values * values, axis=-1, keepdims=True) + EPSILON)
    return values / length, length


def dot(a, b, contract=(1, 0)):
    return lax.dot_general(
        a, b, (((contract[0],), (contract[1],)), ((), ())), preferred_element_type=F32
    )


def halves(values):
    high = values.astype(LOW)
    return high, (values - high.astype(F32)).astype(LOW)


def dot3(a, b, contract=(1, 0)):
    return (
        dot(a[0], b[1], contract) + dot(a[1], b[0], contract)
    ) + dot(a[0], b[0], contract)


def eye():
    shape = (ROWS, ROWS)
    return lax.broadcasted_iota(jnp.int32, shape, 0) == lax.broadcasted_iota(jnp.int32, shape, 1)


def to_row(column):
    return jnp.sum(jnp.where(eye(), column, 0.0), axis=0, keepdims=True)


def to_column(row):
    return jnp.sum(jnp.where(eye(), row, 0.0), axis=1, keepdims=True)


def own_plane(planes):
    return lax.rem(lax.axis_index("dp"), planes)


def own_core():
    return lax.rem(lax.axis_index("blk"), 2)


def prepare(planes, *refs):
    sources, msg_refs, refs = refs[:4], refs[4 : 4 + planes], refs[4 + planes :]
    high_ref, buffers, pick_ref, sems = refs[0], refs[1:5], refs[5], refs[6]
    copies = [
        pltpu.make_async_copy(source, buffer, sems.at[i])
        for i, (source, buffer) in enumerate(zip(sources, buffers))
    ]
    for copy in copies:
        copy.start()
    for copy in copies:
        copy.wait()
    prog_ref, trace_ref, owner_ref, row_ref = buffers
    feat = prog_ref.shape[1]
    neg = owner_ref.shape[0]
    prog_unit, _ = normalize(prog_ref[...])
    trace_unit, _ = normalize(trace_ref[...])
    prog_high = prog_unit.astype(LOW)
    high_ref[...] = trace_unit.astype(LOW)
    pos = to_row(SCALE * jnp.sum(prog_unit * trace_unit, axis=-1, keepdims=True))
    high = pos.astype(LOW).astype(F32)
    mid = (pos - high).astype(LOW).astype(F32)
    last = pos - high - mid
    line = lax.broadcasted_iota(jnp.int32, (8, ROWS), 0)
    pos_tile = jnp.where(line == 0, high, jnp.where(line == 1, mid, jnp.where(line == 2, last, 0.0)))
    owners = owner_ref[...]
    rows = row_ref[...].astype(F32) + 1.0
    line = lax.broadcasted_iota(jnp.int32, (planes * 8, ROWS), 0)
    x, h, c = (lax.shift_right_logical(line, bit) & 1 for bit in range(3))
    index = (planes * h + lax.shift_right_logical(line, 3)) * 4 + 2 * x + c
    picks = jnp.zeros((planes * 8, ROWS), F32)
    for n in range(neg):
        picks = picks + jnp.where(index == owners[n : n + 1, :], rows[n : n + 1, :], 0.0)
    pick_ref[...] = picks
    plane = own_plane(planes)
    rest = jnp.zeros((8, feat - 2 * ROWS), F32)
    for k, msg_ref in enumerate(msg_refs):
        at = pl.multiple_of(8 * (plane ^ k), 8)
        aux = jnp.concatenate([pick_ref[pl.ds(at, 8), :], pos_tile, rest], axis=1)
        msg_ref[0:ROWS, :] = prog_high
        msg_ref[ROWS:, :] = aux.astype(LOW)


def group_parts(prog_ref, trace_ref, *refs):
    _, refs[-1][0:ROWS, :] = halves(normalize(trace_ref[...])[0])
    refs[-1][ROWS : 2 * ROWS, :], refs[-1][2 * ROWS :, :] = halves(normalize(prog_ref[...])[0])


def stack_programs(planes, *refs):
    msgs, out_ref = refs[:planes], refs[planes]
    for k, msg in enumerate(msgs):
        out_ref[k * ROWS : (k + 1) * ROWS, :] = msg[0:ROWS, :]
    aux = jnp.concatenate([msg[ROWS:, :].astype(F32) for msg in msgs], axis=0)
    out_ref[planes * ROWS :, :] = aux.astype(LOW)


def stack_traces(*refs):
    for i, ref in enumerate(refs[:-1]):
        refs[-1][i * ROWS : (i + 1) * ROWS, :] = ref[...]


def found(scores, picks, slots):
    below = lax.broadcasted_iota(jnp.int32, (ROWS, scores.shape[1]), 0).astype(F32) + 1.0
    exps = []
    for i, q in enumerate(slots):
        pick = picks[q : q + 1, :]
        block = scores[i * ROWS : (i + 1) * ROWS, :]
        score = jnp.sum(jnp.where(below == pick, block, 0.0), axis=0, keepdims=True)
        exps.append(jnp.where(pick > 0.0, jnp.exp(SCALE * score), 0.0))
    return exps


def score_near(planes, own_ref, other_ref, near_own, near_other, exp_ref, pick_ref, pos_ref):
    side = planes * ROWS
    for at, stack in ((0, own_ref), (side, other_ref)):
        aux = stack[side:, :].astype(F32)
        for k in range(planes):
            lanes = slice(at + k * ROWS, at + (k + 1) * ROWS)
            tile = aux[8 * k : 8 * k + 8, :]
            pick_ref[:, lanes] = by_slot(planes, tile[:, 0:ROWS])
            pos = tile[:, ROWS : 2 * ROWS]
            pos_ref[:, lanes] = pos[0:1, :] + pos[1:2, :] + pos[2:3, :]
    zero = jnp.zeros((1, side), F32)
    for at, stack in ((0, own_ref), (side, other_ref)):
        lanes = slice(at, at + side)
        exps = []
        for first, near in ((0, near_own), (4, near_other)):
            scores = dot(near[...], stack[0:side, :], (1, 1))
            exps += found(scores, pick_ref[:, lanes], range(first, first + 3)) + [zero]
        exp_ref[:, lanes] = jnp.concatenate(exps, axis=0)


def score_far(planes, exp_in, pick_ref, own_ref, other_ref, far_own, far_other, exp_ref, sum_ref):
    side = planes * ROWS
    plane, core = own_plane(planes), own_core()
    far = jnp.concatenate([far_own[...], far_other[...]], axis=0)
    line = lax.broadcasted_iota(jnp.int32, (8, side), 0)
    for c, stack in enumerate((own_ref, other_ref)):
        lanes = slice(c * side, (c + 1) * side)
        scores = dot(far, stack[0:side, :], (1, 1))
        three, seven = found(scores, pick_ref[:, lanes], (3, 7))
        exps = jnp.where(line == 3, three, jnp.where(line == 7, seven, exp_in[:, lanes]))
        exp_ref[:, lanes] = exps
        sums = jnp.sum(exps, axis=0, keepdims=True)
        for k in range(planes):
            lane = block_lane(planes, c * planes + k, plane, core)
            sum_ref[:, pl.ds(lane, ROWS)] = sums[:, k * ROWS : (k + 1) * ROWS]


def by_slot(planes, picks):
    blk = lax.axis_index("blk")
    bits = (lax.div(blk, 2), lax.div(lax.axis_index("dp"), planes), lax.rem(blk, 2))
    for step, bit in zip((1, 2, 4), bits):
        turned = []
        for at in range(0, 8, 2 * step):
            turned += [picks[at + step : at + 2 * step, :], picks[at : at + step, :]]
        picks = jnp.where(bit == 1, jnp.concatenate(turned, axis=0), picks)
    return picks


def block_lane(planes, b, plane, core):
    return pl.multiple_of((2 * (plane ^ (b % planes)) + (core ^ (b // planes))) * ROWS, ROWS)


def program_terms(planes, exp_ref, pick_ref, near_own, far_own, near_other, far_other, _, *refs):
    mark_ref, own_ref, *out_refs = refs
    side = planes * ROWS
    exps, picks = jnp.transpose(exp_ref[:, 0:side]), jnp.transpose(pick_ref[:, 0:side])
    lanes = lax.broadcasted_iota(jnp.int32, (side, ROWS), 1).astype(F32) + 1.0
    values = jnp.concatenate(
        [
            jnp.where(lanes == picks[:, q : q + 1], exps[:, q : q + 1], 0.0).astype(LOW)
            for q in range(8)
        ],
        axis=1,
    )
    traces = [ref[...] for ref in (near_own, far_own, near_other, far_other)]
    total = dot(values, jnp.concatenate(traces, axis=0))
    mark_ref[...] = total[0:8, 0:ROWS]
    own_ref[...] = total[0:ROWS, :]
    for k, out_ref in enumerate(out_refs, 1):
        out_ref[...] = total[k * ROWS : (k + 1) * ROWS, :].astype(LOW)


def far_terms(planes, exp_ref, pick_ref, pos_ref, own_stack, other_stack, _, *refs):
    sums, (total_ref, weight_ref, far_ref) = refs[:planes], refs[planes:]
    plane, core = own_plane(planes), own_core()
    for b in range(2 * planes):
        lanes = slice(b * ROWS, (b + 1) * ROWS)
        lane = block_lane(planes, b, plane, core)
        total = jnp.exp(pos_ref[:, lanes])
        for one in sums:
            total = total + one[:, pl.ds(lane, ROWS)]
        if b == 0:
            total_ref[...] = total
        weight_ref[:, lanes] = exp_ref[:, lanes] * (SCALE / total)
    far_ref[...] = weighted(planes, weight_ref, pick_ref, own_stack, other_stack, (3,)).astype(LOW)


def weighted(planes, weight_ref, pick_ref, own_stack, other_stack, slots):
    side = planes * ROWS
    below = lax.broadcasted_iota(jnp.int32, (ROWS, side), 0).astype(F32) + 1.0
    result = 0.0
    for at, stack in ((0, own_stack), (side, other_stack)):
        weights = weight_ref[:, at : at + side]
        high = weights.astype(LOW).astype(F32)
        for part in (high, weights - high):
            rows = [
                jnp.where(below == pick_ref[q : q + 1, at : at + side], part[q : q + 1, :], 0.0)
                for q in slots
            ]
            result = result + dot(jnp.concatenate(rows, axis=0).astype(LOW), stack[0:side, :])
    return result


def near_terms(planes, weight_ref, pick_ref, own_stack, other_stack, own_ref, x_ref, h_ref):
    result = weighted(planes, weight_ref, pick_ref, own_stack, other_stack, (0, 1, 2))
    own_ref[...] = result[0:ROWS, :]
    x_ref[...] = result[ROWS : 2 * ROWS, :].astype(LOW)
    h_ref[...] = result[2 * ROWS :, :]


def added(own_ref, other_ref, x_ref, out_ref, x_out):
    out_ref[...] = (own_ref[...] + other_ref[...].astype(F32)).astype(LOW)
    x_out[...] = x_ref[...]


def group_terms(*refs):
    nears, groups, (programs, traces, total_ref, trace_own) = refs[:2], refs[2:4], refs[4:8]
    prog_base, trace_base, prog_out, trace_out, size_ref, loss_ref = refs[8:]

    def part(which):
        at = [(x * 3 + which) * ROWS for x in range(2)]
        return jnp.concatenate([g[a : a + ROWS, :] for a in at for g in groups], axis=0)

    highs = [n[x * ROWS : (x + 1) * ROWS, :] for x in range(2) for n in nears]
    trace = (jnp.concatenate(highs, axis=0), part(0))
    prog = (part(1), part(2))
    scores = SCALE * dot3(prog, trace, (1, 1))
    exps = jnp.exp(scores)
    total = jnp.sum(exps, axis=1, keepdims=True)
    weights = exps / total
    prog_unit, prog_len = normalize(programs[...])
    trace_unit, trace_len = normalize(traces[...])
    prog_out[...] = prog_unit
    trace_out[...] = trace_unit
    pos = SCALE * jnp.sum(prog_unit * trace_unit, axis=-1, keepdims=True)
    hard_total = to_column(total_ref[...])
    pull = jnp.exp(pos) / hard_total - 2.0
    lane = lax.broadcasted_iota(jnp.int32, (ROWS, ROWS), 1)
    sizes = jnp.where(lane == 0, prog_len, jnp.where(lane == 1, trace_len, SCALE / hard_total))
    size_ref[...] = sizes
    group_prog = dot3(halves(weights[0:ROWS, :]), trace)
    prog_base[...] = SCALE * (group_prog + pull * trace_unit)
    group_trace = dot3(halves(jnp.transpose(weights[:, 0:ROWS])), prog)
    trace_base[...] = SCALE * (group_trace + pull * prog_unit) + trace_own[...]
    loss_ref[...] = to_row(jnp.log(total[0:ROWS, :]) - 2.0 * pos) + jnp.log(total_ref[...])


def finish(planes, prog_base, trace_base, prog_unit, trace_unit, size_ref, *refs):
    progs, traces, (prog_out, trace_out) = refs[:planes], refs[planes : planes + 2], refs[planes + 2 :]
    back = trace_base[...]
    for one in traces:
        back = back + one[...].astype(F32)
    hard = progs[0][...]
    for one in progs[1:]:
        hard = hard + one[...].astype(F32)
    direction = prog_base[...] + size_ref[:, 2:3] * hard
    for unit, towards, length, out in (
        (prog_unit[...], direction, size_ref[:, 0:1], prog_out),
        (trace_unit[...], back, size_ref[:, 1:2], trace_out),
    ):
        along = jnp.sum(unit * towards, axis=-1, keepdims=True)
        out[...] = (towards - unit * along) / length


def call(body, outs, flops, moved, scratch=(), in_specs=None, limit=VMEM_LIMIT):
    return pl.pallas_call(
        body,
        out_shape=[jax.ShapeDtypeStruct(shape, dtype) for shape, dtype in outs],
        scratch_shapes=list(scratch),
        **({"in_specs": in_specs} if in_specs else {}),
        compiler_params=pltpu.CompilerParams(vmem_limit_bytes=limit),
        cost_estimate=pl.CostEstimate(flops=flops, bytes_accessed=moved, transcendentals=0),
    )


def joined(own_ref, x_ref, _, out_ref):
    out_ref[0 : 3 * ROWS, :] = own_ref[...]
    out_ref[3 * ROWS :, :] = x_ref[...]


def on_device(dp_count, blk_count, programs, traces, hard_owner, hard_row):
    rows, feat = programs.shape
    planes = dp_count // 2
    size = dp_count * blk_count
    both = ("dp", "blk")

    def flipped(value, bits):
        return lax.ppermute(value, both, [(i, i ^ bits) for i in range(size)])

    def to_plane(value, k):
        return flipped(value, k * blk_count)

    x_bit, h_bit = 2, planes * blk_count
    block = rows * feat
    shape, side, width = (rows, feat), planes * rows, 2 * planes * rows
    hbm = pl.BlockSpec(memory_space=pltpu.HBM)
    index = hard_owner.shape[::-1]
    *sent, high = call(
        functools.partial(prepare, planes),
        [((rows + 8, feat), LOW)] * planes + [(shape, LOW)],
        10 * block,
        20 * block,
        [
            pltpu.VMEM(shape, F32),
            pltpu.VMEM(shape, F32),
            pltpu.VMEM(index, jnp.int32),
            pltpu.VMEM(index, jnp.int32),
            pltpu.VMEM((8 * planes, rows), F32),
            pltpu.SemaphoreType.DMA((4,)),
        ],
        [hbm] * 4,
        None,
    )(programs, traces, hard_owner.T, hard_row.T)
    high_h = flipped(high, h_bit)
    far_first = list(range(planes - 1, 0, -1))
    arrived = [to_plane(sent[k], k) for k in far_first]
    stack = call(
        functools.partial(stack_programs, planes), [((side + 8 * planes, feat), LOW)], STACK, 0
    )(sent[0], *arrived[::-1])[0]
    high_h = call(stack_traces, [(shape, LOW)], HALF, 0)(high_h)[0]
    high_x, far = flipped(high, x_bit), flipped(high_h, x_bit)
    far = call(stack_traces, [(shape, LOW)], FAR, 0)(far)[0]
    near = call(stack_traces, [((3 * rows, feat), LOW)], TRACE, 0)(high, high_x, high_h)[0]
    group = call(group_parts, [((3 * rows, feat), LOW)], 10 * block, 20 * block)(
        programs, traces, high_h
    )[0]
    group_x = flipped(group, x_bit)
    other_stack, other_near, other_far = (flipped(one, 1) for one in (stack, near, far))
    stacks = stack, other_stack

    lists = [((8, width), F32), ((8, width), F32), ((1, width), F32)]
    exps, picks, pos = call(functools.partial(score_near, planes), lists, NEAR, 0)(
        *stacks, near, other_near
    )
    exps, sums = call(functools.partial(score_far, planes), lists[1:], LAST, 0)(
        exps, picks, *stacks, far, other_far
    )
    all_sums = [sums] + [to_plane(sums, k) for k in far_first]

    mark, prog_own, *prog_parts = call(
        functools.partial(program_terms, planes),
        [((8, rows), F32), (shape, F32)] + [(shape, LOW)] * (planes - 1),
        AHEAD,
        0,
    )(exps, picks, near, far, other_near, other_far, sums)
    total, weights, part_xh = call(
        functools.partial(far_terms, planes), [((1, rows), F32), lists[0], (shape, LOW)], 0, 0
    )(exps, picks, pos, *stacks, mark, *all_sums)
    trace_own, part_x, part_h = call(
        functools.partial(near_terms, planes),
        [(shape, F32), (shape, LOW), (shape, F32)],
        12 * rows * width * feat,
        4 * width * feat,
    )(weights, picks, *stacks)
    for_h, part_x = call(added, [(shape, LOW)] * 2, block, 4 * block)(
        part_h, flipped(part_xh, x_bit), part_x
    )
    trace_back = [flipped(for_h, h_bit), flipped(part_x, x_bit)]

    groups = call(joined, [((6 * rows, feat), LOW)], JOIN, 0)(group, group_x, total)[0]
    prog_back = [to_plane(part, k) for k, part in enumerate(prog_parts, 1)]
    *bases, loss = call(
        group_terms,
        [(shape, F32)] * 4 + [((rows, rows), F32), ((1, rows), F32)],
        block,
        block,
    )(near, other_near, groups, flipped(groups, 1), programs, traces, total, trace_own)

    grad_programs, grad_traces = call(
        functools.partial(finish, planes), [(shape, F32)] * 2, block, block
    )(*bases, prog_own, *prog_back, *trace_back)
    return grad_programs, grad_traces, loss.reshape(rows)


def solution(mesh):
    spec = P(("dp", "blk"), None)
    return jax.shard_map(
        functools.partial(on_device, mesh.shape["dp"], mesh.shape["blk"]),
        mesh=mesh,
        in_specs=(spec,) * 4,
        out_specs=(spec, spec, P(("dp", "blk"))),
        check_vma=False,
    )
```

```python
import functools

import jax
import jax.numpy as jnp
from jax import lax
from jax.experimental import pallas as pl
from jax.experimental.pallas import tpu as pltpu
from jax.sharding import PartitionSpec as P

EPSILON = 1e-06
SCALE = 14.0
LOW = jnp.bfloat16
F32 = jnp.float32
ROWS = 128
MORE = 16
AHEAD = 2 * 10**9
NEAR = 10**8
FAR = 5*10**9
HALF = 2*10**9
STACK = 0
TRACE = 4*10**9
LAST = 3*10**8
JOIN = 0
VMEM_LIMIT = 40 * 1024 * 1024


def normalize(values):
    length = jnp.sqrt(jnp.sum(values * values, axis=-1, keepdims=True) + EPSILON)
    return values / length, length


def dot(a, b, contract=(1, 0)):
    return lax.dot_general(
        a, b, (((contract[0],), (contract[1],)), ((), ())), preferred_element_type=F32
    )


def halves(values):
    high = values.astype(LOW)
    return high, (values - high.astype(F32)).astype(LOW)


def dot3(a, b, contract=(1, 0)):
    return (
        dot(a[0], b[1], contract) + dot(a[1], b[0], contract)
    ) + dot(a[0], b[0], contract)


def eye():
    shape = (ROWS, ROWS)
    return lax.broadcasted_iota(jnp.int32, shape, 0) == lax.broadcasted_iota(jnp.int32, shape, 1)


def to_row(column):
    return jnp.sum(jnp.where(eye(), column, 0.0), axis=0, keepdims=True)


def to_column(row):
    return jnp.sum(jnp.where(eye(), row, 0.0), axis=1, keepdims=True)


def own_plane(planes):
    return lax.rem(lax.axis_index("dp"), planes)


def own_core():
    return lax.rem(lax.axis_index("blk"), 2)


def prepare(planes, *refs):
    sources, msg_refs, refs = refs[:4], refs[4 : 4 + planes], refs[4 + planes :]
    high_ref, buffers, pick_ref, sems = refs[0], refs[1:5], refs[5], refs[6]
    copies = [
        pltpu.make_async_copy(source, buffer, sems.at[i])
        for i, (source, buffer) in enumerate(zip(sources, buffers))
    ]
    for copy in copies:
        copy.start()
    for copy in copies:
        copy.wait()
    prog_ref, trace_ref, owner_ref, row_ref = buffers
    feat = prog_ref.shape[1]
    neg = owner_ref.shape[0]
    prog_unit, _ = normalize(prog_ref[...])
    trace_unit, _ = normalize(trace_ref[...])
    prog_high = prog_unit.astype(LOW)
    high_ref[...] = trace_unit.astype(LOW)
    pos = to_row(SCALE * jnp.sum(prog_unit * trace_unit, axis=-1, keepdims=True))
    high = pos.astype(LOW).astype(F32)
    mid = (pos - high).astype(LOW).astype(F32)
    last = pos - high - mid
    line = lax.broadcasted_iota(jnp.int32, (8, ROWS), 0)
    pos_tile = jnp.where(line == 0, high, jnp.where(line == 1, mid, jnp.where(line == 2, last, 0.0)))
    owners = owner_ref[...]
    rows = row_ref[...].astype(F32) + 1.0
    line = lax.broadcasted_iota(jnp.int32, (planes * 8, ROWS), 0)
    x, h, c = (lax.shift_right_logical(line, bit) & 1 for bit in range(3))
    index = (planes * h + lax.shift_right_logical(line, 3)) * 4 + 2 * x + c
    picks = jnp.zeros((planes * 8, ROWS), F32)
    for n in range(neg):
        picks = picks + jnp.where(index == owners[n : n + 1, :], rows[n : n + 1, :], 0.0)
    pick_ref[...] = picks
    plane = own_plane(planes)
    rest = jnp.zeros((8, feat - 2 * ROWS), F32)
    blank = jnp.zeros((MORE - 8, feat), F32)
    for k, msg_ref in enumerate(msg_refs):
        at = pl.multiple_of(8 * (plane ^ k), 8)
        aux = jnp.concatenate([pick_ref[pl.ds(at, 8), :], pos_tile, rest], axis=1)
        msg_ref[0:ROWS, :] = prog_high
        msg_ref[ROWS:, :] = jnp.concatenate([aux, blank], axis=0).astype(LOW)


def group_parts(prog_ref, trace_ref, *refs):
    _, refs[-1][0:ROWS, :] = halves(normalize(trace_ref[...])[0])
    refs[-1][ROWS : 2 * ROWS, :], refs[-1][2 * ROWS :, :] = halves(normalize(prog_ref[...])[0])


def stack_programs(planes, *refs):
    msgs, out_ref = refs[:planes], refs[planes]
    for k, msg in enumerate(msgs):
        out_ref[k * ROWS : (k + 1) * ROWS, :] = msg[0:ROWS, :]
    aux = jnp.concatenate([msg[ROWS:, :].astype(F32)[0:8, :] for msg in msgs], axis=0)
    out_ref[planes * ROWS :, :] = aux.astype(LOW)


def stack_traces(*refs):
    for i, ref in enumerate(refs[:-1]):
        refs[-1][i * ROWS : (i + 1) * ROWS, :] = ref[...]


def found(scores, picks, slots):
    below = lax.broadcasted_iota(jnp.int32, (ROWS, scores.shape[1]), 0).astype(F32) + 1.0
    exps = []
    for i, q in enumerate(slots):
        pick = picks[q : q + 1, :]
        block = scores[i * ROWS : (i + 1) * ROWS, :]
        score = jnp.sum(jnp.where(below == pick, block, 0.0), axis=0, keepdims=True)
        exps.append(jnp.where(pick > 0.0, jnp.exp(SCALE * score), 0.0))
    return exps


def score_near(planes, own_ref, other_ref, near_own, near_other, exp_ref, pick_ref, pos_ref):
    side = planes * ROWS
    for at, stack in ((0, own_ref), (side, other_ref)):
        aux = stack[side:, :].astype(F32)
        for k in range(planes):
            lanes = slice(at + k * ROWS, at + (k + 1) * ROWS)
            tile = aux[8 * k : 8 * k + 8, :]
            pick_ref[:, lanes] = by_slot(planes, tile[:, 0:ROWS])
            pos = tile[:, ROWS : 2 * ROWS]
            pos_ref[:, lanes] = pos[0:1, :] + pos[1:2, :] + pos[2:3, :]
    zero = jnp.zeros((1, side), F32)
    for at, stack in ((0, own_ref), (side, other_ref)):
        lanes = slice(at, at + side)
        exps = []
        for first, near in ((0, near_own), (4, near_other)):
            scores = dot(near[...], stack[0:side, :], (1, 1))
            exps += found(scores, pick_ref[:, lanes], range(first, first + 3)) + [zero]
        exp_ref[:, lanes] = jnp.concatenate(exps, axis=0)


def score_far(planes, exp_in, pick_ref, own_ref, other_ref, far_own, far_other, exp_ref, sum_ref):
    side = planes * ROWS
    plane, core = own_plane(planes), own_core()
    far = jnp.concatenate([far_own[...], far_other[...]], axis=0)
    line = lax.broadcasted_iota(jnp.int32, (8, side), 0)
    for c, stack in enumerate((own_ref, other_ref)):
        lanes = slice(c * side, (c + 1) * side)
        scores = dot(far, stack[0:side, :], (1, 1))
        three, seven = found(scores, pick_ref[:, lanes], (3, 7))
        exps = jnp.where(line == 3, three, jnp.where(line == 7, seven, exp_in[:, lanes]))
        exp_ref[:, lanes] = exps
        sums = jnp.sum(exps, axis=0, keepdims=True)
        for k in range(planes):
            lane = block_lane(planes, c * planes + k, plane, core)
            sum_ref[:, pl.ds(lane, ROWS)] = sums[:, k * ROWS : (k + 1) * ROWS]


def by_slot(planes, picks):
    blk = lax.axis_index("blk")
    bits = (lax.div(blk, 2), lax.div(lax.axis_index("dp"), planes), lax.rem(blk, 2))
    for step, bit in zip((1, 2, 4), bits):
        turned = []
        for at in range(0, 8, 2 * step):
            turned += [picks[at + step : at + 2 * step, :], picks[at : at + step, :]]
        picks = jnp.where(bit == 1, jnp.concatenate(turned, axis=0), picks)
    return picks


def block_lane(planes, b, plane, core):
    return pl.multiple_of((2 * (plane ^ (b % planes)) + (core ^ (b // planes))) * ROWS, ROWS)


def program_terms(planes, exp_ref, pick_ref, near_own, far_own, near_other, far_other, _, *refs):
    mark_ref, own_ref, *out_refs = refs
    side = planes * ROWS
    exps, picks = jnp.transpose(exp_ref[:, 0:side]), jnp.transpose(pick_ref[:, 0:side])
    lanes = lax.broadcasted_iota(jnp.int32, (side, ROWS), 1).astype(F32) + 1.0
    values = jnp.concatenate(
        [
            jnp.where(lanes == picks[:, q : q + 1], exps[:, q : q + 1], 0.0).astype(LOW)
            for q in range(8)
        ],
        axis=1,
    )
    traces = [ref[...] for ref in (near_own, far_own, near_other, far_other)]
    total = dot(values, jnp.concatenate(traces, axis=0))
    mark_ref[...] = total[0:8, 0:ROWS]
    own_ref[...] = total[0:ROWS, :]
    for k, out_ref in enumerate(out_refs, 1):
        out_ref[...] = total[k * ROWS : (k + 1) * ROWS, :].astype(LOW)


def far_terms(planes, exp_ref, pick_ref, pos_ref, own_stack, other_stack, _, *refs):
    sums, (total_ref, weight_ref, far_ref) = refs[:planes], refs[planes:]
    plane, core = own_plane(planes), own_core()
    for b in range(2 * planes):
        lanes = slice(b * ROWS, (b + 1) * ROWS)
        lane = block_lane(planes, b, plane, core)
        total = jnp.exp(pos_ref[:, lanes])
        for one in sums:
            total = total + one[:, pl.ds(lane, ROWS)]
        if b == 0:
            total_ref[...] = total
        weight_ref[:, lanes] = exp_ref[:, lanes] * (SCALE / total)
    far_ref[...] = weighted(planes, weight_ref, pick_ref, own_stack, other_stack, (3,)).astype(LOW)


def weighted(planes, weight_ref, pick_ref, own_stack, other_stack, slots):
    side = planes * ROWS
    below = lax.broadcasted_iota(jnp.int32, (ROWS, side), 0).astype(F32) + 1.0
    result = 0.0
    for at, stack in ((0, own_stack), (side, other_stack)):
        weights = weight_ref[:, at : at + side]
        high = weights.astype(LOW).astype(F32)
        for part in (high, weights - high):
            rows = [
                jnp.where(below == pick_ref[q : q + 1, at : at + side], part[q : q + 1, :], 0.0)
                for q in slots
            ]
            result = result + dot(jnp.concatenate(rows, axis=0).astype(LOW), stack[0:side, :])
    return result


def near_terms(planes, weight_ref, pick_ref, own_stack, other_stack, own_ref, x_ref, h_ref):
    result = weighted(planes, weight_ref, pick_ref, own_stack, other_stack, (0, 1, 2))
    own_ref[...] = result[0:ROWS, :]
    x_ref[...] = result[ROWS : 2 * ROWS, :].astype(LOW)
    h_ref[...] = result[2 * ROWS :, :]


def added(own_ref, other_ref, x_ref, out_ref, x_out):
    out_ref[...] = (own_ref[...] + other_ref[...].astype(F32)).astype(LOW)
    x_out[...] = x_ref[...]


def group_terms(*refs):
    nears, groups, (programs, traces, total_ref, trace_own) = refs[:2], refs[2:4], refs[4:8]
    prog_base, trace_base, prog_out, trace_out, size_ref, loss_ref = refs[8:]

    def part(which):
        at = [(x * 3 + which) * ROWS for x in range(2)]
        return jnp.concatenate([g[a : a + ROWS, :] for a in at for g in groups], axis=0)

    highs = [n[x * ROWS : (x + 1) * ROWS, :] for x in range(2) for n in nears]
    trace = (jnp.concatenate(highs, axis=0), part(0))
    prog = (part(1), part(2))
    scores = SCALE * dot3(prog, trace, (1, 1))
    exps = jnp.exp(scores)
    total = jnp.sum(exps, axis=1, keepdims=True)
    weights = exps / total
    prog_unit, prog_len = normalize(programs[...])
    trace_unit, trace_len = normalize(traces[...])
    prog_out[...] = prog_unit
    trace_out[...] = trace_unit
    pos = SCALE * jnp.sum(prog_unit * trace_unit, axis=-1, keepdims=True)
    hard_total = to_column(total_ref[...])
    pull = jnp.exp(pos) / hard_total - 2.0
    lane = lax.broadcasted_iota(jnp.int32, (ROWS, ROWS), 1)
    sizes = jnp.where(lane == 0, prog_len, jnp.where(lane == 1, trace_len, SCALE / hard_total))
    size_ref[...] = sizes
    group_prog = dot3(halves(weights[0:ROWS, :]), trace)
    prog_base[...] = SCALE * (group_prog + pull * trace_unit)
    group_trace = dot3(halves(jnp.transpose(weights[:, 0:ROWS])), prog)
    trace_base[...] = SCALE * (group_trace + pull * prog_unit) + trace_own[...]
    loss_ref[...] = to_row(jnp.log(total[0:ROWS, :]) - 2.0 * pos) + jnp.log(total_ref[...])


def finish(planes, prog_base, trace_base, prog_unit, trace_unit, size_ref, *refs):
    progs, traces, (prog_out, trace_out) = refs[:planes], refs[planes : planes + 2], refs[planes + 2 :]
    back = trace_base[...]
    for one in traces:
        back = back + one[...].astype(F32)
    hard = progs[0][...]
    for one in progs[1:]:
        hard = hard + one[...].astype(F32)
    direction = prog_base[...] + size_ref[:, 2:3] * hard
    for unit, towards, length, out in (
        (prog_unit[...], direction, size_ref[:, 0:1], prog_out),
        (trace_unit[...], back, size_ref[:, 1:2], trace_out),
    ):
        along = jnp.sum(unit * towards, axis=-1, keepdims=True)
        out[...] = (towards - unit * along) / length


def call(body, outs, flops, moved, scratch=(), in_specs=None, limit=VMEM_LIMIT):
    return pl.pallas_call(
        body,
        out_shape=[jax.ShapeDtypeStruct(shape, dtype) for shape, dtype in outs],
        scratch_shapes=list(scratch),
        **({"in_specs": in_specs} if in_specs else {}),
        compiler_params=pltpu.CompilerParams(vmem_limit_bytes=limit),
        cost_estimate=pl.CostEstimate(flops=flops, bytes_accessed=moved, transcendentals=0),
    )


def joined(own_ref, x_ref, _, out_ref):
    out_ref[0 : 3 * ROWS, :] = own_ref[...]
    out_ref[3 * ROWS :, :] = x_ref[...]


def on_device(dp_count, blk_count, programs, traces, hard_owner, hard_row):
    rows, feat = programs.shape
    planes = dp_count // 2
    size = dp_count * blk_count
    both = ("dp", "blk")

    def flipped(value, bits):
        return lax.ppermute(value, both, [(i, i ^ bits) for i in range(size)])

    def to_plane(value, k):
        return flipped(value, k * blk_count)

    x_bit, h_bit = 2, planes * blk_count
    block = rows * feat
    shape, side, width = (rows, feat), planes * rows, 2 * planes * rows
    hbm = pl.BlockSpec(memory_space=pltpu.HBM)
    index = hard_owner.shape[::-1]
    *sent, high = call(
        functools.partial(prepare, planes),
        [((rows + MORE, feat), LOW)] * planes + [(shape, LOW)],
        10 * block,
        20 * block,
        [
            pltpu.VMEM(shape, F32),
            pltpu.VMEM(shape, F32),
            pltpu.VMEM(index, jnp.int32),
            pltpu.VMEM(index, jnp.int32),
            pltpu.VMEM((8 * planes, rows), F32),
            pltpu.SemaphoreType.DMA((4,)),
        ],
        [hbm] * 4,
        None,
    )(programs, traces, hard_owner.T, hard_row.T)
    high_h = flipped(high, h_bit)
    far_first = list(range(planes - 1, 0, -1))
    arrived = [to_plane(sent[k], k) for k in far_first]
    stack = call(
        functools.partial(stack_programs, planes), [((side + 8 * planes, feat), LOW)], STACK, 0
    )(sent[0], *arrived[::-1])[0]
    high_h = call(stack_traces, [(shape, LOW)], HALF, 0)(high_h)[0]
    high_x, far = flipped(high, x_bit), flipped(high_h, x_bit)
    far = call(stack_traces, [(shape, LOW)], FAR, 0)(far)[0]
    near = call(stack_traces, [((3 * rows, feat), LOW)], TRACE, 0)(high, high_x, high_h)[0]
    group = call(group_parts, [((3 * rows, feat), LOW)], 10 * block, 20 * block)(
        programs, traces, high_h
    )[0]
    group_x = flipped(group, x_bit)
    other_stack, other_near, other_far = (flipped(one, 1) for one in (stack, near, far))
    stacks = stack, other_stack

    lists = [((8, width), F32), ((8, width), F32), ((1, width), F32)]
    exps, picks, pos = call(functools.partial(score_near, planes), lists, NEAR, 0)(
        *stacks, near, other_near
    )
    exps, sums = call(functools.partial(score_far, planes), lists[1:], LAST, 0)(
        exps, picks, *stacks, far, other_far
    )
    all_sums = [sums] + [to_plane(sums, k) for k in far_first]

    mark, prog_own, *prog_parts = call(
        functools.partial(program_terms, planes),
        [((8, rows), F32), (shape, F32)] + [(shape, LOW)] * (planes - 1),
        AHEAD,
        0,
    )(exps, picks, near, far, other_near, other_far, sums)
    total, weights, part_xh = call(
        functools.partial(far_terms, planes), [((1, rows), F32), lists[0], (shape, LOW)], 0, 0
    )(exps, picks, pos, *stacks, mark, *all_sums)
    trace_own, part_x, part_h = call(
        functools.partial(near_terms, planes),
        [(shape, F32), (shape, LOW), (shape, F32)],
        12 * rows * width * feat,
        4 * width * feat,
    )(weights, picks, *stacks)
    for_h, part_x = call(added, [(shape, LOW)] * 2, block, 4 * block)(
        part_h, flipped(part_xh, x_bit), part_x
    )
    trace_back = [flipped(for_h, h_bit), flipped(part_x, x_bit)]

    groups = call(joined, [((6 * rows, feat), LOW)], JOIN, 0)(group, group_x, total)[0]
    prog_back = [to_plane(part, k) for k, part in enumerate(prog_parts, 1)]
    *bases, loss = call(
        group_terms,
        [(shape, F32)] * 4 + [((rows, rows), F32), ((1, rows), F32)],
        block,
        block,
    )(near, other_near, groups, flipped(groups, 1), programs, traces, total, trace_own)

    grad_programs, grad_traces = call(
        functools.partial(finish, planes), [(shape, F32)] * 2, block, block
    )(*bases, prog_own, *prog_back, *trace_back)
    return grad_programs, grad_traces, loss.reshape(rows)


def solution(mesh):
    spec = P(("dp", "blk"), None)
    return jax.shard_map(
        functools.partial(on_device, mesh.shape["dp"], mesh.shape["blk"]),
        mesh=mesh,
        in_specs=(spec,) * 4,
        out_specs=(spec, spec, P(("dp", "blk"))),
        check_vma=False,
    )
```

```python
import functools

import jax
import jax.numpy as jnp
from jax import lax
from jax.experimental import pallas as pl
from jax.experimental.pallas import tpu as pltpu
from jax.sharding import PartitionSpec as P

EPSILON = 1e-06
SCALE = 14.0
LOW = jnp.bfloat16
F32 = jnp.float32
ROWS = 128
MORE = 16
AHEAD = 2 * 10**9
NEAR = 10**8
FAR = 5*10**9
HALF = 2*10**9
STACK = 0
TRACE = 4*10**9
LAST = 3*10**8
JOIN = 0
VMEM_LIMIT = 40 * 1024 * 1024


def normalize(values):
    length = jnp.sqrt(jnp.sum(values * values, axis=-1, keepdims=True) + EPSILON)
    return values / length, length


def dot(a, b, contract=(1, 0)):
    return lax.dot_general(
        a, b, (((contract[0],), (contract[1],)), ((), ())), preferred_element_type=F32
    )


def halves(values):
    high = values.astype(LOW)
    return high, (values - high.astype(F32)).astype(LOW)


def dot3(a, b, contract=(1, 0)):
    return (
        dot(a[0], b[1], contract) + dot(a[1], b[0], contract)
    ) + dot(a[0], b[0], contract)


def eye():
    shape = (ROWS, ROWS)
    return lax.broadcasted_iota(jnp.int32, shape, 0) == lax.broadcasted_iota(jnp.int32, shape, 1)


def to_row(column):
    return jnp.sum(jnp.where(eye(), column, 0.0), axis=0, keepdims=True)


def to_column(row):
    return jnp.sum(jnp.where(eye(), row, 0.0), axis=1, keepdims=True)


def own_plane(planes):
    return lax.rem(lax.axis_index("dp"), planes)


def own_core():
    return lax.rem(lax.axis_index("blk"), 2)


def prepare(planes, *refs):
    sources, msg_refs, refs = refs[:4], refs[4 : 4 + planes], refs[4 + planes :]
    high_ref, buffers, pick_ref, sems = refs[0], refs[1:5], refs[5], refs[6]
    copies = [
        pltpu.make_async_copy(source, buffer, sems.at[i])
        for i, (source, buffer) in enumerate(zip(sources, buffers))
    ]
    for copy in copies:
        copy.start()
    for copy in copies:
        copy.wait()
    prog_ref, trace_ref, owner_ref, row_ref = buffers
    feat = prog_ref.shape[1]
    neg = owner_ref.shape[0]
    prog_unit, _ = normalize(prog_ref[...])
    trace_unit, _ = normalize(trace_ref[...])
    prog_high = prog_unit.astype(LOW)
    high_ref[...] = trace_unit.astype(LOW)
    pos = to_row(SCALE * jnp.sum(prog_unit * trace_unit, axis=-1, keepdims=True))
    high = pos.astype(LOW).astype(F32)
    mid = (pos - high).astype(LOW).astype(F32)
    last = pos - high - mid
    line = lax.broadcasted_iota(jnp.int32, (8, ROWS), 0)
    pos_tile = jnp.where(line == 0, high, jnp.where(line == 1, mid, jnp.where(line == 2, last, 0.0)))
    owners = owner_ref[...]
    rows = row_ref[...].astype(F32) + 1.0
    line = lax.broadcasted_iota(jnp.int32, (planes * 8, ROWS), 0)
    x, h, c = (lax.shift_right_logical(line, bit) & 1 for bit in range(3))
    index = (planes * h + lax.shift_right_logical(line, 3)) * 4 + 2 * x + c
    picks = jnp.zeros((planes * 8, ROWS), F32)
    for n in range(neg):
        picks = picks + jnp.where(index == owners[n : n + 1, :], rows[n : n + 1, :], 0.0)
    pick_ref[...] = picks
    plane = own_plane(planes)
    rest = jnp.zeros((8, feat - 2 * ROWS), F32)
    blank = jnp.zeros((MORE - 8, feat), F32)
    for k, msg_ref in enumerate(msg_refs):
        at = pl.multiple_of(8 * (plane ^ k), 8)
        aux = jnp.concatenate([pick_ref[pl.ds(at, 8), :], pos_tile, rest], axis=1)
        msg_ref[0:ROWS, :] = prog_high
        msg_ref[ROWS:, :] = jnp.concatenate([aux, blank], axis=0).astype(LOW)


def group_parts(prog_ref, trace_ref, *refs):
    _, refs[-1][0:ROWS, :] = halves(normalize(trace_ref[...])[0])
    refs[-1][ROWS : 2 * ROWS, :], refs[-1][2 * ROWS :, :] = halves(normalize(prog_ref[...])[0])


def stack_programs(planes, *refs):
    msgs, out_ref = refs[:planes], refs[planes]
    for k, msg in enumerate(msgs):
        out_ref[k * ROWS : (k + 1) * ROWS, :] = msg[0:ROWS, :]
    aux = jnp.concatenate([msg[ROWS:, :].astype(F32)[0:8, :] for msg in msgs], axis=0)
    out_ref[planes * ROWS :, :] = aux.astype(LOW)


def stack_traces(*refs):
    for i, ref in enumerate(refs[:-1]):
        refs[-1][i * ROWS : (i + 1) * ROWS, :] = ref[...]


def found(scores, picks, slots):
    below = lax.broadcasted_iota(jnp.int32, (ROWS, scores.shape[1]), 0).astype(F32) + 1.0
    exps = []
    for i, q in enumerate(slots):
        pick = picks[q : q + 1, :]
        block = scores[i * ROWS : (i + 1) * ROWS, :]
        score = jnp.sum(jnp.where(below == pick, block, 0.0), axis=0, keepdims=True)
        exps.append(jnp.where(pick > 0.0, jnp.exp(SCALE * score), 0.0))
    return exps


def score_near(planes, own_ref, other_ref, near_own, near_other, exp_ref, pick_ref, pos_ref):
    side = planes * ROWS
    for at, stack in ((0, own_ref), (side, other_ref)):
        aux = stack[side:, :].astype(F32)
        for k in range(planes):
            lanes = slice(at + k * ROWS, at + (k + 1) * ROWS)
            tile = aux[8 * k : 8 * k + 8, :]
            pick_ref[:, lanes] = by_slot(planes, tile[:, 0:ROWS])
            pos = tile[:, ROWS : 2 * ROWS]
            pos_ref[:, lanes] = pos[0:1, :] + pos[1:2, :] + pos[2:3, :]
    zero = jnp.zeros((1, side), F32)
    for at, stack in ((0, own_ref), (side, other_ref)):
        lanes = slice(at, at + side)
        exps = []
        for first, near in ((0, near_own), (4, near_other)):
            scores = dot(near[...], stack[0:side, :], (1, 1))
            exps += found(scores, pick_ref[:, lanes], range(first, first + 3)) + [zero]
        exp_ref[:, lanes] = jnp.concatenate(exps, axis=0)


def score_far(planes, exp_in, pick_ref, own_ref, other_ref, far_own, far_other, exp_ref, sum_ref):
    side = planes * ROWS
    plane, core = own_plane(planes), own_core()
    far = jnp.concatenate([far_own[...], far_other[...]], axis=0)
    line = lax.broadcasted_iota(jnp.int32, (8, side), 0)
    for c, stack in enumerate((own_ref, other_ref)):
        lanes = slice(c * side, (c + 1) * side)
        scores = dot(far, stack[0:side, :], (1, 1))
        three, seven = found(scores, pick_ref[:, lanes], (3, 7))
        exps = jnp.where(line == 3, three, jnp.where(line == 7, seven, exp_in[:, lanes]))
        exp_ref[:, lanes] = exps
        sums = jnp.sum(exps, axis=0, keepdims=True)
        for k in range(planes):
            lane = block_lane(planes, c * planes + k, plane, core)
            sum_ref[:, pl.ds(lane, ROWS)] = sums[:, k * ROWS : (k + 1) * ROWS]


def by_slot(planes, picks):
    blk = lax.axis_index("blk")
    bits = (lax.div(blk, 2), lax.div(lax.axis_index("dp"), planes), lax.rem(blk, 2))
    for step, bit in zip((1, 2, 4), bits):
        turned = []
        for at in range(0, 8, 2 * step):
            turned += [picks[at + step : at + 2 * step, :], picks[at : at + step, :]]
        picks = jnp.where(bit == 1, jnp.concatenate(turned, axis=0), picks)
    return picks


def block_lane(planes, b, plane, core):
    return pl.multiple_of((2 * (plane ^ (b % planes)) + (core ^ (b // planes))) * ROWS, ROWS)


def program_terms(planes, exp_ref, pick_ref, near_own, far_own, near_other, far_other, _, *refs):
    mark_ref, own_ref, *out_refs = refs
    side = planes * ROWS
    exps, picks = jnp.transpose(exp_ref[:, 0:side]), jnp.transpose(pick_ref[:, 0:side])
    lanes = lax.broadcasted_iota(jnp.int32, (side, ROWS), 1).astype(F32) + 1.0
    values = jnp.concatenate(
        [
            jnp.where(lanes == picks[:, q : q + 1], exps[:, q : q + 1], 0.0).astype(LOW)
            for q in range(8)
        ],
        axis=1,
    )
    traces = [ref[...] for ref in (near_own, far_own, near_other, far_other)]
    total = dot(values, jnp.concatenate(traces, axis=0))
    mark_ref[...] = total[0:8, 0:ROWS]
    own_ref[...] = total[0:ROWS, :]
    for k, out_ref in enumerate(out_refs, 1):
        out_ref[...] = total[k * ROWS : (k + 1) * ROWS, :].astype(LOW)


def far_terms(planes, exp_ref, pick_ref, pos_ref, own_stack, other_stack, _, *refs):
    sums, (total_ref, weight_ref, far_ref) = refs[:planes], refs[planes:]
    plane, core = own_plane(planes), own_core()
    for b in range(2 * planes):
        lanes = slice(b * ROWS, (b + 1) * ROWS)
        lane = block_lane(planes, b, plane, core)
        total = jnp.exp(pos_ref[:, lanes])
        for one in sums:
            total = total + one[:, pl.ds(lane, ROWS)]
        if b == 0:
            total_ref[...] = total
        weight_ref[:, lanes] = exp_ref[:, lanes] * (SCALE / total)
    far_ref[...] = weighted(planes, weight_ref, pick_ref, own_stack, other_stack, (3,)).astype(LOW)


def weighted(planes, weight_ref, pick_ref, own_stack, other_stack, slots):
    side = planes * ROWS
    below = lax.broadcasted_iota(jnp.int32, (ROWS, side), 0).astype(F32) + 1.0
    result = 0.0
    for at, stack in ((0, own_stack), (side, other_stack)):
        weights = weight_ref[:, at : at + side]
        high = weights.astype(LOW).astype(F32)
        for part in (high, weights - high):
            rows = [
                jnp.where(below == pick_ref[q : q + 1, at : at + side], part[q : q + 1, :], 0.0)
                for q in slots
            ]
            result = result + dot(jnp.concatenate(rows, axis=0).astype(LOW), stack[0:side, :])
    return result


def near_terms(planes, weight_ref, pick_ref, own_stack, other_stack, own_ref, x_ref, h_ref):
    result = weighted(planes, weight_ref, pick_ref, own_stack, other_stack, (0, 1, 2))
    own_ref[...] = result[0:ROWS, :]
    x_ref[...] = result[ROWS : 2 * ROWS, :].astype(LOW)
    h_ref[...] = result[2 * ROWS :, :]


def added(own_ref, other_ref, x_ref, out_ref, x_out):
    out_ref[...] = (own_ref[...] + other_ref[...].astype(F32)).astype(LOW)
    x_out[...] = x_ref[...]


def group_terms(*refs):
    nears, groups, (programs, traces, total_ref, trace_own) = refs[:2], refs[2:4], refs[4:8]
    prog_base, trace_base, prog_out, trace_out, size_ref, loss_ref = refs[8:]

    def part(which):
        at = [(x * 3 + which) * ROWS for x in range(2)]
        return jnp.concatenate([g[a : a + ROWS, :] for a in at for g in groups], axis=0)

    highs = [n[x * ROWS : (x + 1) * ROWS, :] for x in range(2) for n in nears]
    trace = (jnp.concatenate(highs, axis=0), part(0))
    prog = (part(1), part(2))
    scores = SCALE * dot3(prog, trace, (1, 1))
    exps = jnp.exp(scores)
    total = jnp.sum(exps, axis=1, keepdims=True)
    weights = exps / total
    prog_unit, prog_len = normalize(programs[...])
    trace_unit, trace_len = normalize(traces[...])
    prog_out[...] = prog_unit
    trace_out[...] = trace_unit
    pos = SCALE * jnp.sum(prog_unit * trace_unit, axis=-1, keepdims=True)
    hard_total = to_column(total_ref[...])
    pull = jnp.exp(pos) / hard_total - 2.0
    lane = lax.broadcasted_iota(jnp.int32, (ROWS, ROWS), 1)
    sizes = jnp.where(lane == 0, prog_len, jnp.where(lane == 1, trace_len, SCALE / hard_total))
    size_ref[...] = sizes
    group_prog = dot3(halves(weights[0:ROWS, :]), trace)
    prog_base[...] = SCALE * (group_prog + pull * trace_unit)
    group_trace = dot3(halves(jnp.transpose(weights[:, 0:ROWS])), prog)
    trace_base[...] = SCALE * (group_trace + pull * prog_unit) + trace_own[...]
    loss_ref[...] = to_row(jnp.log(total[0:ROWS, :]) - 2.0 * pos) + jnp.log(total_ref[...])


def finish(planes, prog_base, trace_base, prog_unit, trace_unit, size_ref, *refs):
    progs, traces, (prog_out, trace_out) = refs[:planes], refs[planes : planes + 2], refs[planes + 2 :]
    back = trace_base[...]
    for one in traces:
        back = back + one[...].astype(F32)
    hard = progs[0][...]
    for one in progs[1:]:
        hard = hard + one[...].astype(F32)
    direction = prog_base[...] + size_ref[:, 2:3] * hard
    for unit, towards, length, out in (
        (prog_unit[...], direction, size_ref[:, 0:1], prog_out),
        (trace_unit[...], back, size_ref[:, 1:2], trace_out),
    ):
        along = jnp.sum(unit * towards, axis=-1, keepdims=True)
        out[...] = (towards - unit * along) / length


def call(body, outs, flops, moved, scratch=(), in_specs=None, limit=VMEM_LIMIT):
    return pl.pallas_call(
        body,
        out_shape=[jax.ShapeDtypeStruct(shape, dtype) for shape, dtype in outs],
        scratch_shapes=list(scratch),
        **({"in_specs": in_specs} if in_specs else {}),
        compiler_params=pltpu.CompilerParams(vmem_limit_bytes=limit),
        cost_estimate=pl.CostEstimate(flops=flops, bytes_accessed=moved, transcendentals=0),
    )


def joined(own_ref, x_ref, _, out_ref):
    out_ref[0 : 3 * ROWS, :] = own_ref[...]
    out_ref[3 * ROWS :, :] = x_ref[...]


def on_device(dp_count, blk_count, programs, traces, hard_owner, hard_row):
    rows, feat = programs.shape
    planes = dp_count // 2
    size = dp_count * blk_count
    both = ("dp", "blk")

    def flipped(value, bits):
        return lax.ppermute(value, both, [(i, i ^ bits) for i in range(size)])

    def to_plane(value, k):
        return flipped(value, k * blk_count)

    x_bit, h_bit = 2, planes * blk_count
    block = rows * feat
    shape, side, width = (rows, feat), planes * rows, 2 * planes * rows
    hbm = pl.BlockSpec(memory_space=pltpu.HBM)
    index = hard_owner.shape[::-1]
    *sent, high = call(
        functools.partial(prepare, planes),
        [((rows + MORE, feat), LOW)] * planes + [(shape, LOW)],
        10 * block,
        20 * block,
        [
            pltpu.VMEM(shape, F32),
            pltpu.VMEM(shape, F32),
            pltpu.VMEM(index, jnp.int32),
            pltpu.VMEM(index, jnp.int32),
            pltpu.VMEM((8 * planes, rows), F32),
            pltpu.SemaphoreType.DMA((4,)),
        ],
        [hbm] * 4,
        None,
    )(programs, traces, hard_owner.T, hard_row.T)
    high_h = flipped(high, h_bit)
    far_first = list(range(planes - 1, 0, -1))
    arrived = [to_plane(sent[k], k) for k in far_first]
    stack = call(
        functools.partial(stack_programs, planes), [((side + 8 * planes, feat), LOW)], STACK, 0
    )(sent[0], *arrived[::-1])[0]
    high_h = call(stack_traces, [(shape, LOW)], HALF, 0)(high_h)[0]
    high_x, far = flipped(high, x_bit), flipped(high_h, x_bit)
    far = call(stack_traces, [(shape, LOW)], FAR, 0)(far)[0]
    near = call(stack_traces, [((3 * rows, feat), LOW)], TRACE, 0)(high, high_x, high_h)[0]
    group = call(group_parts, [((3 * rows, feat), LOW)], 10 * block, 20 * block)(
        programs, traces, high_h
    )[0]
    group_x = flipped(group, x_bit)
    other_stack, other_near, other_far = (flipped(one, 1) for one in (stack, near, far))
    stacks = stack, other_stack

    lists = [((8, width), F32), ((8, width), F32), ((1, width), F32)]
    exps, picks, pos = call(functools.partial(score_near, planes), lists, NEAR, 0)(
        *stacks, near, other_near
    )
    exps, sums = call(functools.partial(score_far, planes), lists[1:], LAST, 0)(
        exps, picks, *stacks, far, other_far
    )
    all_sums = [sums] + [to_plane(sums, k) for k in [2] + [k for k in far_first if k != 2]]

    mark, prog_own, *prog_parts = call(
        functools.partial(program_terms, planes),
        [((8, rows), F32), (shape, F32)] + [(shape, LOW)] * (planes - 1),
        AHEAD,
        0,
    )(exps, picks, near, far, other_near, other_far, sums)
    total, weights, part_xh = call(
        functools.partial(far_terms, planes), [((1, rows), F32), lists[0], (shape, LOW)], 0, 0
    )(exps, picks, pos, *stacks, mark, *all_sums)
    trace_own, part_x, part_h = call(
        functools.partial(near_terms, planes),
        [(shape, F32), (shape, LOW), (shape, F32)],
        12 * rows * width * feat,
        4 * width * feat,
    )(weights, picks, *stacks)
    for_h, part_x = call(added, [(shape, LOW)] * 2, block, 4 * block)(
        part_h, flipped(part_xh, x_bit), part_x
    )
    trace_back = [flipped(for_h, h_bit), flipped(part_x, x_bit)]

    groups = call(joined, [((6 * rows, feat), LOW)], JOIN, 0)(group, group_x, total)[0]
    prog_back = [to_plane(part, k) for k, part in enumerate(prog_parts, 1)]
    *bases, loss = call(
        group_terms,
        [(shape, F32)] * 4 + [((rows, rows), F32), ((1, rows), F32)],
        block,
        block,
    )(near, other_near, groups, flipped(groups, 1), programs, traces, total, trace_own)

    grad_programs, grad_traces = call(
        functools.partial(finish, planes), [(shape, F32)] * 2, block, block
    )(*bases, prog_own, *prog_back, *trace_back)
    return grad_programs, grad_traces, loss.reshape(rows)


def solution(mesh):
    spec = P(("dp", "blk"), None)
    return jax.shard_map(
        functools.partial(on_device, mesh.shape["dp"], mesh.shape["blk"]),
        mesh=mesh,
        in_specs=(spec,) * 4,
        out_specs=(spec, spec, P(("dp", "blk"))),
        check_vma=False,
    )
```

```python
import functools

import jax
import jax.numpy as jnp
from jax import lax
from jax.experimental import pallas as pl
from jax.experimental.pallas import tpu as pltpu
from jax.sharding import PartitionSpec as P

EPSILON = 1e-06
SCALE = 14.0
LOW = jnp.bfloat16
F32 = jnp.float32
ROWS = 128
MORE = 16
AHEAD = 2 * 10**9
NEAR = 10**8
FAR = 5*10**9
HALF = 2*10**9
STACK = 0
TRACE = 4*10**9
LAST = 3*10**8
JOIN = 0
VMEM_LIMIT = 40 * 1024 * 1024


def normalize(values):
    length = jnp.sqrt(jnp.sum(values * values, axis=-1, keepdims=True) + EPSILON)
    return values / length, length


def dot(a, b, contract=(1, 0)):
    return lax.dot_general(
        a, b, (((contract[0],), (contract[1],)), ((), ())), preferred_element_type=F32
    )


def halves(values):
    high = values.astype(LOW)
    return high, (values - high.astype(F32)).astype(LOW)


def dot3(a, b, contract=(1, 0)):
    return (
        dot(a[0], b[1], contract) + dot(a[1], b[0], contract)
    ) + dot(a[0], b[0], contract)


def eye():
    shape = (ROWS, ROWS)
    return lax.broadcasted_iota(jnp.int32, shape, 0) == lax.broadcasted_iota(jnp.int32, shape, 1)


def to_row(column):
    return jnp.sum(jnp.where(eye(), column, 0.0), axis=0, keepdims=True)


def to_column(row):
    return jnp.sum(jnp.where(eye(), row, 0.0), axis=1, keepdims=True)


def own_plane(planes):
    return lax.rem(lax.axis_index("dp"), planes)


def own_core():
    return lax.rem(lax.axis_index("blk"), 2)


def prepare(planes, *refs):
    sources, msg_refs, refs = refs[:4], refs[4 : 4 + planes], refs[4 + planes :]
    high_ref, buffers, pick_ref, sems = refs[0], refs[1:5], refs[5], refs[6]
    copies = [
        pltpu.make_async_copy(source, buffer, sems.at[i])
        for i, (source, buffer) in enumerate(zip(sources, buffers))
    ]
    for copy in copies:
        copy.start()
    for copy in copies:
        copy.wait()
    prog_ref, trace_ref, owner_ref, row_ref = buffers
    feat = prog_ref.shape[1]
    neg = owner_ref.shape[0]
    prog_unit, _ = normalize(prog_ref[...])
    trace_unit, _ = normalize(trace_ref[...])
    prog_high = prog_unit.astype(LOW)
    high_ref[...] = trace_unit.astype(LOW)
    pos = to_row(SCALE * jnp.sum(prog_unit * trace_unit, axis=-1, keepdims=True))
    high = pos.astype(LOW).astype(F32)
    mid = (pos - high).astype(LOW).astype(F32)
    last = pos - high - mid
    line = lax.broadcasted_iota(jnp.int32, (8, ROWS), 0)
    pos_tile = jnp.where(line == 0, high, jnp.where(line == 1, mid, jnp.where(line == 2, last, 0.0)))
    owners = owner_ref[...]
    rows = row_ref[...].astype(F32) + 1.0
    line = lax.broadcasted_iota(jnp.int32, (planes * 8, ROWS), 0)
    x, h, c = (lax.shift_right_logical(line, bit) & 1 for bit in range(3))
    index = (planes * h + lax.shift_right_logical(line, 3)) * 4 + 2 * x + c
    picks = jnp.zeros((planes * 8, ROWS), F32)
    for n in range(neg):
        picks = picks + jnp.where(index == owners[n : n + 1, :], rows[n : n + 1, :], 0.0)
    pick_ref[...] = picks
    plane = own_plane(planes)
    rest = jnp.zeros((8, feat - 2 * ROWS), F32)
    blank = jnp.zeros((MORE - 8, feat), F32)
    for k, msg_ref in enumerate(msg_refs):
        at = pl.multiple_of(8 * (plane ^ k), 8)
        aux = jnp.concatenate([pick_ref[pl.ds(at, 8), :], pos_tile, rest], axis=1)
        msg_ref[0:ROWS, :] = prog_high
        msg_ref[ROWS:, :] = jnp.concatenate([aux, blank], axis=0).astype(LOW)


def group_parts(prog_ref, trace_ref, *refs):
    _, refs[-1][0:ROWS, :] = halves(normalize(trace_ref[...])[0])
    refs[-1][ROWS : 2 * ROWS, :], refs[-1][2 * ROWS :, :] = halves(normalize(prog_ref[...])[0])


def stack_programs(planes, *refs):
    msgs, out_ref = refs[:planes], refs[planes]
    for k, msg in enumerate(msgs):
        out_ref[k * ROWS : (k + 1) * ROWS, :] = msg[0:ROWS, :]
    aux = jnp.concatenate([msg[ROWS:, :].astype(F32)[0:8, :] for msg in msgs], axis=0)
    out_ref[planes * ROWS :, :] = aux.astype(LOW)


def stack_traces(*refs):
    for i, ref in enumerate(refs[:-1]):
        refs[-1][i * ROWS : (i + 1) * ROWS, :] = ref[...]


def found(scores, picks, slots):
    below = lax.broadcasted_iota(jnp.int32, (ROWS, scores.shape[1]), 0).astype(F32) + 1.0
    exps = []
    for i, q in enumerate(slots):
        pick = picks[q : q + 1, :]
        block = scores[i * ROWS : (i + 1) * ROWS, :]
        score = jnp.sum(jnp.where(below == pick, block, 0.0), axis=0, keepdims=True)
        exps.append(jnp.where(pick > 0.0, jnp.exp(SCALE * score), 0.0))
    return exps


def score_near(planes, own_ref, other_ref, near_own, near_other, exp_ref, pick_ref, pos_ref):
    side = planes * ROWS
    for at, stack in ((0, own_ref), (side, other_ref)):
        aux = stack[side:, :].astype(F32)
        for k in range(planes):
            lanes = slice(at + k * ROWS, at + (k + 1) * ROWS)
            tile = aux[8 * k : 8 * k + 8, :]
            pick_ref[:, lanes] = by_slot(planes, tile[:, 0:ROWS])
            pos = tile[:, ROWS : 2 * ROWS]
            pos_ref[:, lanes] = pos[0:1, :] + pos[1:2, :] + pos[2:3, :]
    zero = jnp.zeros((1, side), F32)
    for at, stack in ((0, own_ref), (side, other_ref)):
        lanes = slice(at, at + side)
        exps = []
        for first, near in ((0, near_own), (4, near_other)):
            scores = dot(near[...], stack[0:side, :], (1, 1))
            exps += found(scores, pick_ref[:, lanes], range(first, first + 3)) + [zero]
        exp_ref[:, lanes] = jnp.concatenate(exps, axis=0)


def score_far(planes, exp_in, pick_ref, own_ref, other_ref, far_own, far_other, exp_ref, sum_ref):
    side = planes * ROWS
    plane, core = own_plane(planes), own_core()
    far = jnp.concatenate([far_own[...], far_other[...]], axis=0)
    line = lax.broadcasted_iota(jnp.int32, (8, side), 0)
    for c, stack in enumerate((own_ref, other_ref)):
        lanes = slice(c * side, (c + 1) * side)
        scores = dot(far, stack[0:side, :], (1, 1))
        three, seven = found(scores, pick_ref[:, lanes], (3, 7))
        exps = jnp.where(line == 3, three, jnp.where(line == 7, seven, exp_in[:, lanes]))
        exp_ref[:, lanes] = exps
        sums = jnp.sum(exps, axis=0, keepdims=True)
        for k in range(planes):
            lane = block_lane(planes, c * planes + k, plane, core)
            sum_ref[:, pl.ds(lane, ROWS)] = sums[:, k * ROWS : (k + 1) * ROWS]


def by_slot(planes, picks):
    blk = lax.axis_index("blk")
    bits = (lax.div(blk, 2), lax.div(lax.axis_index("dp"), planes), lax.rem(blk, 2))
    for step, bit in zip((1, 2, 4), bits):
        turned = []
        for at in range(0, 8, 2 * step):
            turned += [picks[at + step : at + 2 * step, :], picks[at : at + step, :]]
        picks = jnp.where(bit == 1, jnp.concatenate(turned, axis=0), picks)
    return picks


def block_lane(planes, b, plane, core):
    return pl.multiple_of((2 * (plane ^ (b % planes)) + (core ^ (b // planes))) * ROWS, ROWS)


def program_terms(planes, exp_ref, pick_ref, near_own, far_own, near_other, far_other, _, *refs):
    mark_ref, own_ref, *out_refs = refs
    side = planes * ROWS
    exps, picks = jnp.transpose(exp_ref[:, 0:side]), jnp.transpose(pick_ref[:, 0:side])
    lanes = lax.broadcasted_iota(jnp.int32, (side, ROWS), 1).astype(F32) + 1.0
    values = jnp.concatenate(
        [
            jnp.where(lanes == picks[:, q : q + 1], exps[:, q : q + 1], 0.0).astype(LOW)
            for q in range(8)
        ],
        axis=1,
    )
    traces = [ref[...] for ref in (near_own, far_own, near_other, far_other)]
    total = dot(values, jnp.concatenate(traces, axis=0))
    mark_ref[...] = total[0:8, 0:ROWS]
    own_ref[...] = total[0:ROWS, :]
    for k, out_ref in enumerate(out_refs, 1):
        out_ref[...] = total[k * ROWS : (k + 1) * ROWS, :].astype(LOW)


def far_terms(planes, exp_ref, pick_ref, pos_ref, own_stack, other_stack, _, *refs):
    sums, (total_ref, weight_ref, far_ref) = refs[:planes], refs[planes:]
    plane, core = own_plane(planes), own_core()
    for b in range(2 * planes):
        lanes = slice(b * ROWS, (b + 1) * ROWS)
        lane = block_lane(planes, b, plane, core)
        total = jnp.exp(pos_ref[:, lanes])
        for one in sums:
            total = total + one[:, pl.ds(lane, ROWS)]
        if b == 0:
            total_ref[...] = total
        weight_ref[:, lanes] = exp_ref[:, lanes] * (SCALE / total)
    far_ref[...] = weighted(planes, weight_ref, pick_ref, own_stack, other_stack, (3,)).astype(LOW)


def weighted(planes, weight_ref, pick_ref, own_stack, other_stack, slots):
    side = planes * ROWS
    below = lax.broadcasted_iota(jnp.int32, (ROWS, side), 0).astype(F32) + 1.0
    result = 0.0
    for at, stack in ((0, own_stack), (side, other_stack)):
        weights = weight_ref[:, at : at + side]
        high = weights.astype(LOW).astype(F32)
        for part in (high, weights - high):
            rows = [
                jnp.where(below == pick_ref[q : q + 1, at : at + side], part[q : q + 1, :], 0.0)
                for q in slots
            ]
            result = result + dot(jnp.concatenate(rows, axis=0).astype(LOW), stack[0:side, :])
    return result


def near_terms(planes, weight_ref, pick_ref, own_stack, other_stack, own_ref, x_ref, h_ref):
    result = weighted(planes, weight_ref, pick_ref, own_stack, other_stack, (0, 1, 2))
    own_ref[...] = result[0:ROWS, :]
    x_ref[...] = result[ROWS : 2 * ROWS, :].astype(LOW)
    h_ref[...] = result[2 * ROWS :, :]


def added(own_ref, other_ref, x_ref, out_ref, x_out):
    out_ref[...] = (own_ref[...] + other_ref[...].astype(F32)).astype(LOW)
    x_out[...] = x_ref[...]


def group_terms(*refs):
    nears, groups, (programs, traces, total_ref, trace_own) = refs[:2], refs[2:4], refs[4:8]
    prog_base, trace_base, prog_out, trace_out, size_ref, loss_ref = refs[8:]

    def part(which):
        at = [(x * 3 + which) * ROWS for x in range(2)]
        return jnp.concatenate([g[a : a + ROWS, :] for a in at for g in groups], axis=0)

    highs = [n[x * ROWS : (x + 1) * ROWS, :] for x in range(2) for n in nears]
    trace = (jnp.concatenate(highs, axis=0), part(0))
    prog = (part(1), part(2))
    scores = SCALE * dot3(prog, trace, (1, 1))
    exps = jnp.exp(scores)
    total = jnp.sum(exps, axis=1, keepdims=True)
    weights = exps / total
    prog_unit, prog_len = normalize(programs[...])
    trace_unit, trace_len = normalize(traces[...])
    prog_out[...] = prog_unit
    trace_out[...] = trace_unit
    pos = SCALE * jnp.sum(prog_unit * trace_unit, axis=-1, keepdims=True)
    hard_total = to_column(total_ref[...])
    pull = jnp.exp(pos) / hard_total - 2.0
    lane = lax.broadcasted_iota(jnp.int32, (ROWS, ROWS), 1)
    sizes = jnp.where(lane == 0, prog_len, jnp.where(lane == 1, trace_len, SCALE / hard_total))
    size_ref[...] = sizes
    group_prog = dot3(halves(weights[0:ROWS, :]), trace)
    prog_base[...] = SCALE * (group_prog + pull * trace_unit)
    group_trace = dot3(halves(jnp.transpose(weights[:, 0:ROWS])), prog)
    trace_base[...] = SCALE * (group_trace + pull * prog_unit) + trace_own[...]
    loss_ref[...] = to_row(jnp.log(total[0:ROWS, :]) - 2.0 * pos) + jnp.log(total_ref[...])


def finish(planes, prog_base, trace_base, prog_unit, trace_unit, size_ref, *refs):
    progs, traces, refs = refs[:planes], refs[planes : planes + 2], refs[planes + 2 :]
    results, made, sems = refs[:2], refs[2:4], refs[4]
    copies = [pltpu.make_async_copy(made[i], results[i], sems.at[i]) for i in range(2)]
    back = trace_base[...]
    for one in traces:
        back = back + one[...].astype(F32)
    hard = progs[0][...]
    for one in progs[1:]:
        hard = hard + one[...].astype(F32)
    direction = prog_base[...] + size_ref[:, 2:3] * hard
    for i, (unit, towards) in enumerate(((prog_unit[...], direction), (trace_unit[...], back))):
        along = jnp.sum(unit * towards, axis=-1, keepdims=True)
        made[i][...] = (towards - unit * along) / size_ref[:, i : i + 1]
        copies[i].start()
    for copy in copies:
        copy.wait()


def call(body, outs, flops, moved, scratch=(), in_specs=None, limit=VMEM_LIMIT, out_specs=None):
    return pl.pallas_call(
        body,
        out_shape=[jax.ShapeDtypeStruct(shape, dtype) for shape, dtype in outs],
        scratch_shapes=list(scratch),
        **({"in_specs": in_specs} if in_specs else {}),
        **({"out_specs": out_specs} if out_specs else {}),
        compiler_params=pltpu.CompilerParams(vmem_limit_bytes=limit),
        cost_estimate=pl.CostEstimate(flops=flops, bytes_accessed=moved, transcendentals=0),
    )


def joined(own_ref, x_ref, _, out_ref):
    out_ref[0 : 3 * ROWS, :] = own_ref[...]
    out_ref[3 * ROWS :, :] = x_ref[...]


def on_device(dp_count, blk_count, programs, traces, hard_owner, hard_row):
    rows, feat = programs.shape
    planes = dp_count // 2
    size = dp_count * blk_count
    both = ("dp", "blk")

    def flipped(value, bits):
        return lax.ppermute(value, both, [(i, i ^ bits) for i in range(size)])

    def to_plane(value, k):
        return flipped(value, k * blk_count)

    x_bit, h_bit = 2, planes * blk_count
    block = rows * feat
    shape, side, width = (rows, feat), planes * rows, 2 * planes * rows
    hbm = pl.BlockSpec(memory_space=pltpu.HBM)
    index = hard_owner.shape[::-1]
    *sent, high = call(
        functools.partial(prepare, planes),
        [((rows + MORE, feat), LOW)] * planes + [(shape, LOW)],
        10 * block,
        20 * block,
        [
            pltpu.VMEM(shape, F32),
            pltpu.VMEM(shape, F32),
            pltpu.VMEM(index, jnp.int32),
            pltpu.VMEM(index, jnp.int32),
            pltpu.VMEM((8 * planes, rows), F32),
            pltpu.SemaphoreType.DMA((4,)),
        ],
        [hbm] * 4,
        None,
    )(programs, traces, hard_owner.T, hard_row.T)
    high_h = flipped(high, h_bit)
    far_first = list(range(planes - 1, 0, -1))
    arrived = [to_plane(sent[k], k) for k in far_first]
    stack = call(
        functools.partial(stack_programs, planes), [((side + 8 * planes, feat), LOW)], STACK, 0
    )(sent[0], *arrived[::-1])[0]
    high_h = call(stack_traces, [(shape, LOW)], HALF, 0)(high_h)[0]
    high_x, far = flipped(high, x_bit), flipped(high_h, x_bit)
    far = call(stack_traces, [(shape, LOW)], FAR, 0)(far)[0]
    near = call(stack_traces, [((3 * rows, feat), LOW)], TRACE, 0)(high, high_x, high_h)[0]
    group = call(group_parts, [((3 * rows, feat), LOW)], 10 * block, 20 * block)(
        programs, traces, high_h
    )[0]
    group_x = flipped(group, x_bit)
    other_stack, other_near, other_far = (flipped(one, 1) for one in (stack, near, far))
    stacks = stack, other_stack

    lists = [((8, width), F32), ((8, width), F32), ((1, width), F32)]
    exps, picks, pos = call(functools.partial(score_near, planes), lists, NEAR, 0)(
        *stacks, near, other_near
    )
    exps, sums = call(functools.partial(score_far, planes), lists[1:], LAST, 0)(
        exps, picks, *stacks, far, other_far
    )
    all_sums = [sums] + [to_plane(sums, k) for k in [2] + [k for k in far_first if k != 2]]

    mark, prog_own, *prog_parts = call(
        functools.partial(program_terms, planes),
        [((8, rows), F32), (shape, F32)] + [(shape, LOW)] * (planes - 1),
        AHEAD,
        0,
    )(exps, picks, near, far, other_near, other_far, sums)
    total, weights, part_xh = call(
        functools.partial(far_terms, planes), [((1, rows), F32), lists[0], (shape, LOW)], 0, 0
    )(exps, picks, pos, *stacks, mark, *all_sums)
    trace_own, part_x, part_h = call(
        functools.partial(near_terms, planes),
        [(shape, F32), (shape, LOW), (shape, F32)],
        12 * rows * width * feat,
        4 * width * feat,
    )(weights, picks, *stacks)
    for_h, part_x = call(added, [(shape, LOW)] * 2, block, 4 * block)(
        part_h, flipped(part_xh, x_bit), part_x
    )
    trace_back = [flipped(for_h, h_bit), flipped(part_x, x_bit)]

    groups = call(joined, [((6 * rows, feat), LOW)], JOIN, 0)(group, group_x, total)[0]
    prog_back = [to_plane(prog_parts[k - 1], k) for k in [1] + far_first[:-1]]
    *bases, loss = call(
        group_terms,
        [(shape, F32)] * 4 + [((rows, rows), F32), ((1, rows), F32)],
        block,
        block,
    )(near, other_near, groups, flipped(groups, 1), programs, traces, total, trace_own)

    grad_programs, grad_traces = call(
        functools.partial(finish, planes),
        [(shape, F32)] * 2,
        block,
        block,
        [pltpu.VMEM(shape, F32), pltpu.VMEM(shape, F32), pltpu.SemaphoreType.DMA((2,))],
        None,
        VMEM_LIMIT,
        [hbm] * 2,
    )(*bases, prog_own, *prog_back, *trace_back)
    return grad_programs, grad_traces, loss.reshape(rows)


def solution(mesh):
    spec = P(("dp", "blk"), None)
    return jax.shard_map(
        functools.partial(on_device, mesh.shape["dp"], mesh.shape["blk"]),
        mesh=mesh,
        in_specs=(spec,) * 4,
        out_specs=(spec, spec, P(("dp", "blk"))),
        check_vma=False,
    )
```

```python
import functools

import jax
import jax.numpy as jnp
from jax import lax
from jax.experimental import pallas as pl
from jax.experimental.pallas import tpu as pltpu
from jax.sharding import PartitionSpec as P

EPSILON = 1e-06
SCALE = 14.0
LOW = jnp.bfloat16
F32 = jnp.float32
ROWS = 128
MORE = 16
AHEAD = 2 * 10**9
NEAR = 10**8
FAR = 5*10**9
HALF = 2*10**9
STACK = 0
TRACE = 4*10**9
LAST = 3*10**8
JOIN = 0
VMEM_LIMIT = 40 * 1024 * 1024


def normalize(values):
    length = jnp.sqrt(jnp.sum(values * values, axis=-1, keepdims=True) + EPSILON)
    return values / length, length


def dot(a, b, contract=(1, 0)):
    return lax.dot_general(
        a, b, (((contract[0],), (contract[1],)), ((), ())), preferred_element_type=F32
    )


def halves(values):
    high = values.astype(LOW)
    return high, (values - high.astype(F32)).astype(LOW)


def dot3(a, b, contract=(1, 0)):
    return (
        dot(a[0], b[1], contract) + dot(a[1], b[0], contract)
    ) + dot(a[0], b[0], contract)


def eye():
    shape = (ROWS, ROWS)
    return lax.broadcasted_iota(jnp.int32, shape, 0) == lax.broadcasted_iota(jnp.int32, shape, 1)


def to_row(column):
    return jnp.sum(jnp.where(eye(), column, 0.0), axis=0, keepdims=True)


def to_column(row):
    return jnp.sum(jnp.where(eye(), row, 0.0), axis=1, keepdims=True)


def own_plane(planes):
    return lax.rem(lax.axis_index("dp"), planes)


def own_core():
    return lax.rem(lax.axis_index("blk"), 2)


def prepare(planes, *refs):
    sources, msg_refs, refs = refs[:4], refs[4 : 4 + planes], refs[4 + planes :]
    high_ref, buffers, pick_ref, sems = refs[0], refs[1:5], refs[5], refs[6]
    copies = [
        pltpu.make_async_copy(source, buffer, sems.at[i])
        for i, (source, buffer) in enumerate(zip(sources, buffers))
    ]
    for copy in copies:
        copy.start()
    for copy in copies:
        copy.wait()
    prog_ref, trace_ref, owner_ref, row_ref = buffers
    feat = prog_ref.shape[1]
    neg = owner_ref.shape[0]
    prog_unit, _ = normalize(prog_ref[...])
    trace_unit, _ = normalize(trace_ref[...])
    prog_high = prog_unit.astype(LOW)
    high_ref[...] = trace_unit.astype(LOW)
    pos = to_row(SCALE * jnp.sum(prog_unit * trace_unit, axis=-1, keepdims=True))
    high = pos.astype(LOW).astype(F32)
    mid = (pos - high).astype(LOW).astype(F32)
    last = pos - high - mid
    line = lax.broadcasted_iota(jnp.int32, (8, ROWS), 0)
    pos_tile = jnp.where(line == 0, high, jnp.where(line == 1, mid, jnp.where(line == 2, last, 0.0)))
    owners = owner_ref[...]
    rows = row_ref[...].astype(F32) + 1.0
    line = lax.broadcasted_iota(jnp.int32, (planes * 8, ROWS), 0)
    x, h, c = (lax.shift_right_logical(line, bit) & 1 for bit in range(3))
    index = (planes * h + lax.shift_right_logical(line, 3)) * 4 + 2 * x + c
    picks = jnp.zeros((planes * 8, ROWS), F32)
    for n in range(neg):
        picks = picks + jnp.where(index == owners[n : n + 1, :], rows[n : n + 1, :], 0.0)
    pick_ref[...] = picks
    plane = own_plane(planes)
    rest = jnp.zeros((8, feat - 2 * ROWS), F32)
    blank = jnp.zeros((MORE - 8, feat), F32)
    for k, msg_ref in enumerate(msg_refs):
        at = pl.multiple_of(8 * (plane ^ k), 8)
        aux = jnp.concatenate([pick_ref[pl.ds(at, 8), :], pos_tile, rest], axis=1)
        msg_ref[0:ROWS, :] = prog_high
        msg_ref[ROWS:, :] = jnp.concatenate([aux, blank], axis=0).astype(LOW)


def group_parts(prog_ref, trace_ref, *refs):
    _, refs[-1][0:ROWS, :] = halves(normalize(trace_ref[...])[0])
    refs[-1][ROWS : 2 * ROWS, :], refs[-1][2 * ROWS :, :] = halves(normalize(prog_ref[...])[0])


def stack_programs(planes, *refs):
    msgs, out_ref = refs[:planes], refs[planes]
    for k, msg in enumerate(msgs):
        out_ref[k * ROWS : (k + 1) * ROWS, :] = msg[0:ROWS, :]
    aux = jnp.concatenate([msg[ROWS:, :].astype(F32)[0:8, :] for msg in msgs], axis=0)
    out_ref[planes * ROWS :, :] = aux.astype(LOW)


def stack_traces(*refs):
    for i, ref in enumerate(refs[:-1]):
        refs[-1][i * ROWS : (i + 1) * ROWS, :] = ref[...]


def found(scores, picks, slots):
    below = lax.broadcasted_iota(jnp.int32, (ROWS, scores.shape[1]), 0).astype(F32) + 1.0
    exps = []
    for i, q in enumerate(slots):
        pick = picks[q : q + 1, :]
        block = scores[i * ROWS : (i + 1) * ROWS, :]
        score = jnp.sum(jnp.where(below == pick, block, 0.0), axis=0, keepdims=True)
        exps.append(jnp.where(pick > 0.0, jnp.exp(SCALE * score), 0.0))
    return exps


def score_near(planes, own_ref, other_ref, near_own, near_other, exp_ref, pick_ref, pos_ref):
    side = planes * ROWS
    for at, stack in ((0, own_ref), (side, other_ref)):
        aux = stack[side:, :].astype(F32)
        for k in range(planes):
            lanes = slice(at + k * ROWS, at + (k + 1) * ROWS)
            tile = aux[8 * k : 8 * k + 8, :]
            pick_ref[:, lanes] = by_slot(planes, tile[:, 0:ROWS])
            pos = tile[:, ROWS : 2 * ROWS]
            pos_ref[:, lanes] = pos[0:1, :] + pos[1:2, :] + pos[2:3, :]
    zero = jnp.zeros((1, side), F32)
    for at, stack in ((0, own_ref), (side, other_ref)):
        lanes = slice(at, at + side)
        exps = []
        for first, near in ((0, near_own), (4, near_other)):
            scores = dot(near[...], stack[0:side, :], (1, 1))
            exps += found(scores, pick_ref[:, lanes], range(first, first + 3)) + [zero]
        exp_ref[:, lanes] = jnp.concatenate(exps, axis=0)


def score_far(planes, exp_in, pick_ref, own_ref, other_ref, far_own, far_other, exp_ref, sum_ref):
    side = planes * ROWS
    plane, core = own_plane(planes), own_core()
    far = jnp.concatenate([far_own[...], far_other[...]], axis=0)
    line = lax.broadcasted_iota(jnp.int32, (8, side), 0)
    for c, stack in enumerate((own_ref, other_ref)):
        lanes = slice(c * side, (c + 1) * side)
        scores = dot(far, stack[0:side, :], (1, 1))
        three, seven = found(scores, pick_ref[:, lanes], (3, 7))
        exps = jnp.where(line == 3, three, jnp.where(line == 7, seven, exp_in[:, lanes]))
        exp_ref[:, lanes] = exps
        sums = jnp.sum(exps, axis=0, keepdims=True)
        for k in range(planes):
            lane = block_lane(planes, c * planes + k, plane, core)
            sum_ref[:, pl.ds(lane, ROWS)] = sums[:, k * ROWS : (k + 1) * ROWS]


def by_slot(planes, picks):
    blk = lax.axis_index("blk")
    bits = (lax.div(blk, 2), lax.div(lax.axis_index("dp"), planes), lax.rem(blk, 2))
    for step, bit in zip((1, 2, 4), bits):
        turned = []
        for at in range(0, 8, 2 * step):
            turned += [picks[at + step : at + 2 * step, :], picks[at : at + step, :]]
        picks = jnp.where(bit == 1, jnp.concatenate(turned, axis=0), picks)
    return picks


def block_lane(planes, b, plane, core):
    return pl.multiple_of((2 * (plane ^ (b % planes)) + (core ^ (b // planes))) * ROWS, ROWS)


def program_terms(planes, exp_ref, pick_ref, near_own, far_own, near_other, far_other, _, *refs):
    mark_ref, own_ref, *out_refs = refs
    side = planes * ROWS
    exps, picks = jnp.transpose(exp_ref[:, 0:side]), jnp.transpose(pick_ref[:, 0:side])
    lanes = lax.broadcasted_iota(jnp.int32, (side, ROWS), 1).astype(F32) + 1.0
    values = jnp.concatenate(
        [
            jnp.where(lanes == picks[:, q : q + 1], exps[:, q : q + 1], 0.0).astype(LOW)
            for q in range(8)
        ],
        axis=1,
    )
    traces = [ref[...] for ref in (near_own, far_own, near_other, far_other)]
    total = dot(values, jnp.concatenate(traces, axis=0))
    mark_ref[...] = total[0:8, 0:ROWS]
    own_ref[...] = total[0:ROWS, :]
    for k, out_ref in enumerate(out_refs, 1):
        out_ref[...] = total[k * ROWS : (k + 1) * ROWS, :].astype(LOW)


def far_terms(planes, exp_ref, pick_ref, pos_ref, own_stack, other_stack, _, *refs):
    sums, (total_ref, weight_ref, far_ref) = refs[:planes], refs[planes:]
    plane, core = own_plane(planes), own_core()
    parts, pairs = [], []
    for b in range(2 * planes):
        lane = block_lane(planes, b, plane, core)
        part = sums[0][:, pl.ds(lane, ROWS)]
        for one in sums[1:]:
            part = part + one[:, pl.ds(lane, ROWS)]
        parts.append(part)
        pairs.append(pos_ref[:, b * ROWS : (b + 1) * ROWS])
    total = jnp.exp(jnp.concatenate(pairs, axis=0)) + jnp.concatenate(parts, axis=0)
    total_ref[...] = total[0:1, :]
    scale = SCALE / total
    for b in range(2 * planes):
        lanes = slice(b * ROWS, (b + 1) * ROWS)
        weight_ref[:, lanes] = exp_ref[:, lanes] * scale[b : b + 1, :]
    far_ref[...] = weighted(planes, weight_ref, pick_ref, own_stack, other_stack, (3,)).astype(LOW)


def weighted(planes, weight_ref, pick_ref, own_stack, other_stack, slots):
    side = planes * ROWS
    below = lax.broadcasted_iota(jnp.int32, (ROWS, side), 0).astype(F32) + 1.0
    result = 0.0
    for at, stack in ((0, own_stack), (side, other_stack)):
        weights = weight_ref[:, at : at + side]
        high = weights.astype(LOW).astype(F32)
        for part in (high, weights - high):
            rows = [
                jnp.where(below == pick_ref[q : q + 1, at : at + side], part[q : q + 1, :], 0.0)
                for q in slots
            ]
            result = result + dot(jnp.concatenate(rows, axis=0).astype(LOW), stack[0:side, :])
    return result


def near_terms(planes, weight_ref, pick_ref, own_stack, other_stack, own_ref, x_ref, h_ref):
    result = weighted(planes, weight_ref, pick_ref, own_stack, other_stack, (0, 1, 2))
    own_ref[...] = result[0:ROWS, :]
    x_ref[...] = result[ROWS : 2 * ROWS, :].astype(LOW)
    h_ref[...] = result[2 * ROWS :, :]


def added(own_ref, other_ref, x_ref, out_ref, x_out):
    out_ref[...] = (own_ref[...] + other_ref[...].astype(F32)).astype(LOW)
    x_out[...] = x_ref[...]


def group_terms(*refs):
    nears, groups, (programs, traces, total_ref, trace_own) = refs[:2], refs[2:4], refs[4:8]
    prog_base, trace_base, prog_out, trace_out, size_ref, loss_ref = refs[8:]

    def part(which):
        at = [(x * 3 + which) * ROWS for x in range(2)]
        return jnp.concatenate([g[a : a + ROWS, :] for a in at for g in groups], axis=0)

    highs = [n[x * ROWS : (x + 1) * ROWS, :] for x in range(2) for n in nears]
    trace = (jnp.concatenate(highs, axis=0), part(0))
    prog = (part(1), part(2))
    scores = SCALE * dot3(prog, trace, (1, 1))
    exps = jnp.exp(scores)
    total = jnp.sum(exps, axis=1, keepdims=True)
    weights = exps / total
    prog_unit, prog_len = normalize(programs[...])
    trace_unit, trace_len = normalize(traces[...])
    prog_out[...] = prog_unit
    trace_out[...] = trace_unit
    pos = SCALE * jnp.sum(prog_unit * trace_unit, axis=-1, keepdims=True)
    hard_total = to_column(total_ref[...])
    pull = jnp.exp(pos) / hard_total - 2.0
    lane = lax.broadcasted_iota(jnp.int32, (ROWS, ROWS), 1)
    sizes = jnp.where(lane == 0, prog_len, jnp.where(lane == 1, trace_len, SCALE / hard_total))
    size_ref[...] = sizes
    group_prog = dot3(halves(weights[0:ROWS, :]), trace)
    prog_base[...] = SCALE * (group_prog + pull * trace_unit)
    group_trace = dot3(halves(jnp.transpose(weights[:, 0:ROWS])), prog)
    trace_base[...] = SCALE * (group_trace + pull * prog_unit) + trace_own[...]
    loss_ref[...] = to_row(jnp.log(total[0:ROWS, :]) - 2.0 * pos) + jnp.log(total_ref[...])


def finish(planes, prog_base, trace_base, prog_unit, trace_unit, size_ref, *refs):
    progs, traces, (prog_out, trace_out) = refs[:planes], refs[planes : planes + 2], refs[planes + 2 :]
    back = trace_base[...]
    for one in traces:
        back = back + one[...].astype(F32)
    hard = progs[0][...]
    for one in progs[1:]:
        hard = hard + one[...].astype(F32)
    direction = prog_base[...] + size_ref[:, 2:3] * hard
    for unit, towards, length, out in (
        (prog_unit[...], direction, size_ref[:, 0:1], prog_out),
        (trace_unit[...], back, size_ref[:, 1:2], trace_out),
    ):
        along = jnp.sum(unit * towards, axis=-1, keepdims=True)
        out[...] = (towards - unit * along) / length


def call(body, outs, flops, moved, scratch=(), in_specs=None, limit=VMEM_LIMIT):
    return pl.pallas_call(
        body,
        out_shape=[jax.ShapeDtypeStruct(shape, dtype) for shape, dtype in outs],
        scratch_shapes=list(scratch),
        **({"in_specs": in_specs} if in_specs else {}),
        compiler_params=pltpu.CompilerParams(vmem_limit_bytes=limit),
        cost_estimate=pl.CostEstimate(flops=flops, bytes_accessed=moved, transcendentals=0),
    )


def joined(own_ref, x_ref, _, out_ref):
    out_ref[0 : 3 * ROWS, :] = own_ref[...]
    out_ref[3 * ROWS :, :] = x_ref[...]


def on_device(dp_count, blk_count, programs, traces, hard_owner, hard_row):
    rows, feat = programs.shape
    planes = dp_count // 2
    size = dp_count * blk_count
    both = ("dp", "blk")

    def flipped(value, bits):
        return lax.ppermute(value, both, [(i, i ^ bits) for i in range(size)])

    def to_plane(value, k):
        return flipped(value, k * blk_count)

    x_bit, h_bit = 2, planes * blk_count
    block = rows * feat
    shape, side, width = (rows, feat), planes * rows, 2 * planes * rows
    hbm = pl.BlockSpec(memory_space=pltpu.HBM)
    index = hard_owner.shape[::-1]
    *sent, high = call(
        functools.partial(prepare, planes),
        [((rows + MORE, feat), LOW)] * planes + [(shape, LOW)],
        10 * block,
        20 * block,
        [
            pltpu.VMEM(shape, F32),
            pltpu.VMEM(shape, F32),
            pltpu.VMEM(index, jnp.int32),
            pltpu.VMEM(index, jnp.int32),
            pltpu.VMEM((8 * planes, rows), F32),
            pltpu.SemaphoreType.DMA((4,)),
        ],
        [hbm] * 4,
        None,
    )(programs, traces, hard_owner.T, hard_row.T)
    high_h = flipped(high, h_bit)
    far_first = list(range(planes - 1, 0, -1))
    arrived = [to_plane(sent[k], k) for k in far_first]
    stack = call(
        functools.partial(stack_programs, planes), [((side + 8 * planes, feat), LOW)], STACK, 0
    )(sent[0], *arrived[::-1])[0]
    high_h = call(stack_traces, [(shape, LOW)], HALF, 0)(high_h)[0]
    high_x, far = flipped(high, x_bit), flipped(high_h, x_bit)
    far = call(stack_traces, [(shape, LOW)], FAR, 0)(far)[0]
    near = call(stack_traces, [((3 * rows, feat), LOW)], TRACE, 0)(high, high_x, high_h)[0]
    group = call(group_parts, [((3 * rows, feat), LOW)], 10 * block, 20 * block)(
        programs, traces, high_h
    )[0]
    group_x = flipped(group, x_bit)
    other_stack, other_near, other_far = (flipped(one, 1) for one in (stack, near, far))
    stacks = stack, other_stack

    lists = [((8, width), F32), ((8, width), F32), ((1, width), F32)]
    exps, picks, pos = call(functools.partial(score_near, planes), lists, NEAR, 0)(
        *stacks, near, other_near
    )
    exps, sums = call(functools.partial(score_far, planes), lists[1:], LAST, 0)(
        exps, picks, *stacks, far, other_far
    )
    all_sums = [sums] + [to_plane(sums, k) for k in [2] + [k for k in far_first if k != 2]]

    mark, prog_own, *prog_parts = call(
        functools.partial(program_terms, planes),
        [((8, rows), F32), (shape, F32)] + [(shape, LOW)] * (planes - 1),
        AHEAD,
        0,
    )(exps, picks, near, far, other_near, other_far, sums)
    total, weights, part_xh = call(
        functools.partial(far_terms, planes), [((1, rows), F32), lists[0], (shape, LOW)], 0, 0
    )(exps, picks, pos, *stacks, mark, *all_sums)
    trace_own, part_x, part_h = call(
        functools.partial(near_terms, planes),
        [(shape, F32), (shape, LOW), (shape, F32)],
        12 * rows * width * feat,
        4 * width * feat,
    )(weights, picks, *stacks)
    for_h, part_x = call(added, [(shape, LOW)] * 2, block, 4 * block)(
        part_h, flipped(part_xh, x_bit), part_x
    )
    trace_back = [flipped(for_h, h_bit), flipped(part_x, x_bit)]

    groups = call(joined, [((6 * rows, feat), LOW)], JOIN, 0)(group, group_x, total)[0]
    prog_back = [to_plane(part, k) for k, part in enumerate(prog_parts, 1)]
    *bases, loss = call(
        group_terms,
        [(shape, F32)] * 4 + [((rows, rows), F32), ((1, rows), F32)],
        block,
        block,
    )(near, other_near, groups, flipped(groups, 1), programs, traces, total, trace_own)

    grad_programs, grad_traces = call(
        functools.partial(finish, planes), [(shape, F32)] * 2, block, block
    )(*bases, prog_own, *prog_back, *trace_back)
    return grad_programs, grad_traces, loss.reshape(rows)


def solution(mesh):
    spec = P(("dp", "blk"), None)
    return jax.shard_map(
        functools.partial(on_device, mesh.shape["dp"], mesh.shape["blk"]),
        mesh=mesh,
        in_specs=(spec,) * 4,
        out_specs=(spec, spec, P(("dp", "blk"))),
        check_vma=False,
    )
```

```python
import functools

import jax
import jax.numpy as jnp
from jax import lax
from jax.experimental import pallas as pl
from jax.experimental.pallas import tpu as pltpu
from jax.sharding import PartitionSpec as P

EPSILON = 1e-06
SCALE = 14.0
LOW = jnp.bfloat16
F32 = jnp.float32
ROWS = 128
MORE = 16
AHEAD = 2 * 10**9
NEAR = 10**8
FAR = 5*10**9
HALF = 2*10**9
STACK = 0
TRACE = 4*10**9
LAST = 3*10**8
JOIN = 0
VMEM_LIMIT = 40 * 1024 * 1024


def normalize(values):
    length = jnp.sqrt(jnp.sum(values * values, axis=-1, keepdims=True) + EPSILON)
    return values / length, length


def dot(a, b, contract=(1, 0)):
    return lax.dot_general(
        a, b, (((contract[0],), (contract[1],)), ((), ())), preferred_element_type=F32
    )


def halves(values):
    high = values.astype(LOW)
    return high, (values - high.astype(F32)).astype(LOW)


def dot3(a, b, contract=(1, 0)):
    return (
        dot(a[0], b[1], contract) + dot(a[1], b[0], contract)
    ) + dot(a[0], b[0], contract)


def eye():
    shape = (ROWS, ROWS)
    return lax.broadcasted_iota(jnp.int32, shape, 0) == lax.broadcasted_iota(jnp.int32, shape, 1)


def to_row(column):
    return jnp.sum(jnp.where(eye(), column, 0.0), axis=0, keepdims=True)


def to_column(row):
    return jnp.sum(jnp.where(eye(), row, 0.0), axis=1, keepdims=True)


def own_plane(planes):
    return lax.rem(lax.axis_index("dp"), planes)


def own_core():
    return lax.rem(lax.axis_index("blk"), 2)


def prepare(planes, *refs):
    sources, msg_refs, refs = refs[:4], refs[4 : 4 + planes], refs[4 + planes :]
    high_ref, buffers, pick_ref, sems = refs[0], refs[1:5], refs[5], refs[6]
    copies = [
        pltpu.make_async_copy(source, buffer, sems.at[i])
        for i, (source, buffer) in enumerate(zip(sources, buffers))
    ]
    for copy in copies:
        copy.start()
    for copy in copies:
        copy.wait()
    prog_ref, trace_ref, owner_ref, row_ref = buffers
    feat = prog_ref.shape[1]
    neg = owner_ref.shape[0]
    prog_unit, _ = normalize(prog_ref[...])
    trace_unit, _ = normalize(trace_ref[...])
    prog_high = prog_unit.astype(LOW)
    high_ref[...] = trace_unit.astype(LOW)
    pos = to_row(SCALE * jnp.sum(prog_unit * trace_unit, axis=-1, keepdims=True))
    high = pos.astype(LOW).astype(F32)
    mid = (pos - high).astype(LOW).astype(F32)
    last = pos - high - mid
    line = lax.broadcasted_iota(jnp.int32, (8, ROWS), 0)
    pos_tile = jnp.where(line == 0, high, jnp.where(line == 1, mid, jnp.where(line == 2, last, 0.0)))
    owners = owner_ref[...]
    rows = row_ref[...].astype(F32) + 1.0
    line = lax.broadcasted_iota(jnp.int32, (planes * 8, ROWS), 0)
    x, h, c = (lax.shift_right_logical(line, bit) & 1 for bit in range(3))
    index = (planes * h + lax.shift_right_logical(line, 3)) * 4 + 2 * x + c
    picks = jnp.zeros((planes * 8, ROWS), F32)
    for n in range(neg):
        picks = picks + jnp.where(index == owners[n : n + 1, :], rows[n : n + 1, :], 0.0)
    pick_ref[...] = picks
    plane = own_plane(planes)
    rest = jnp.zeros((8, feat - 2 * ROWS), F32)
    blank = jnp.zeros((MORE - 8, feat), F32)
    for k, msg_ref in enumerate(msg_refs):
        at = pl.multiple_of(8 * (plane ^ k), 8)
        aux = jnp.concatenate([pick_ref[pl.ds(at, 8), :], pos_tile, rest], axis=1)
        msg_ref[0:ROWS, :] = prog_high
        msg_ref[ROWS:, :] = jnp.concatenate([aux, blank], axis=0).astype(LOW)


def group_parts(prog_ref, trace_ref, *refs):
    _, refs[-1][0:ROWS, :] = halves(normalize(trace_ref[...])[0])
    refs[-1][ROWS : 2 * ROWS, :], refs[-1][2 * ROWS :, :] = halves(normalize(prog_ref[...])[0])


def stack_programs(planes, *refs):
    msgs, out_ref = (refs[0], *refs[planes - 1 : 0 : -1]), refs[planes]
    for k, msg in enumerate(msgs):
        out_ref[k * ROWS : (k + 1) * ROWS, :] = msg[0:ROWS, :]
    aux = jnp.concatenate([msg[ROWS:, :].astype(F32)[0:8, :] for msg in msgs], axis=0)
    out_ref[planes * ROWS :, :] = aux.astype(LOW)


def stack_traces(*refs):
    for i, ref in enumerate(refs[:-1]):
        refs[-1][i * ROWS : (i + 1) * ROWS, :] = ref[...]


def found(scores, picks, slots):
    below = lax.broadcasted_iota(jnp.int32, (ROWS, scores.shape[1]), 0).astype(F32) + 1.0
    exps = []
    for i, q in enumerate(slots):
        pick = picks[q : q + 1, :]
        block = scores[i * ROWS : (i + 1) * ROWS, :]
        score = jnp.sum(jnp.where(below == pick, block, 0.0), axis=0, keepdims=True)
        exps.append(jnp.where(pick > 0.0, jnp.exp(SCALE * score), 0.0))
    return exps


def score_near(planes, own_ref, other_ref, near_own, near_other, exp_ref, pick_ref, pos_ref):
    side = planes * ROWS
    for at, stack in ((0, own_ref), (side, other_ref)):
        aux = stack[side:, :].astype(F32)
        for k in range(planes):
            lanes = slice(at + k * ROWS, at + (k + 1) * ROWS)
            tile = aux[8 * k : 8 * k + 8, :]
            pick_ref[:, lanes] = by_slot(planes, tile[:, 0:ROWS])
            pos = tile[:, ROWS : 2 * ROWS]
            pos_ref[:, lanes] = pos[0:1, :] + pos[1:2, :] + pos[2:3, :]
    zero = jnp.zeros((1, side), F32)
    for at, stack in ((0, own_ref), (side, other_ref)):
        lanes = slice(at, at + side)
        exps = []
        for first, near in ((0, near_own), (4, near_other)):
            scores = dot(near[...], stack[0:side, :], (1, 1))
            exps += found(scores, pick_ref[:, lanes], range(first, first + 3)) + [zero]
        exp_ref[:, lanes] = jnp.concatenate(exps, axis=0)


def score_far(planes, exp_in, pick_ref, own_ref, other_ref, far_own, far_other, exp_ref, sum_ref):
    side = planes * ROWS
    plane, core = own_plane(planes), own_core()
    far = jnp.concatenate([far_own[...], far_other[...]], axis=0)
    line = lax.broadcasted_iota(jnp.int32, (8, side), 0)
    for c, stack in enumerate((own_ref, other_ref)):
        lanes = slice(c * side, (c + 1) * side)
        scores = dot(far, stack[0:side, :], (1, 1))
        three, seven = found(scores, pick_ref[:, lanes], (3, 7))
        exps = jnp.where(line == 3, three, jnp.where(line == 7, seven, exp_in[:, lanes]))
        exp_ref[:, lanes] = exps
        sums = jnp.sum(exps, axis=0, keepdims=True)
        for k in range(planes):
            lane = block_lane(planes, c * planes + k, plane, core)
            sum_ref[:, pl.ds(lane, ROWS)] = sums[:, k * ROWS : (k + 1) * ROWS]


def by_slot(planes, picks):
    blk = lax.axis_index("blk")
    bits = (lax.div(blk, 2), lax.div(lax.axis_index("dp"), planes), lax.rem(blk, 2))
    for step, bit in zip((1, 2, 4), bits):
        turned = []
        for at in range(0, 8, 2 * step):
            turned += [picks[at + step : at + 2 * step, :], picks[at : at + step, :]]
        picks = jnp.where(bit == 1, jnp.concatenate(turned, axis=0), picks)
    return picks


def block_lane(planes, b, plane, core):
    return pl.multiple_of((2 * (plane ^ (b % planes)) + (core ^ (b // planes))) * ROWS, ROWS)


def program_terms(planes, exp_ref, pick_ref, near_own, far_own, near_other, far_other, _, *refs):
    mark_ref, own_ref, *out_refs = refs
    side = planes * ROWS
    exps, picks = jnp.transpose(exp_ref[:, 0:side]), jnp.transpose(pick_ref[:, 0:side])
    lanes = lax.broadcasted_iota(jnp.int32, (side, ROWS), 1).astype(F32) + 1.0
    values = jnp.concatenate(
        [
            jnp.where(lanes == picks[:, q : q + 1], exps[:, q : q + 1], 0.0).astype(LOW)
            for q in range(8)
        ],
        axis=1,
    )
    traces = [ref[...] for ref in (near_own, far_own, near_other, far_other)]
    total = dot(values, jnp.concatenate(traces, axis=0))
    mark_ref[...] = total[0:8, 0:ROWS]
    own_ref[...] = total[0:ROWS, :]
    for k, out_ref in enumerate(out_refs, 1):
        out_ref[...] = total[k * ROWS : (k + 1) * ROWS, :].astype(LOW)


def far_terms(planes, exp_ref, pick_ref, pos_ref, own_stack, other_stack, _, *refs):
    sums, (total_ref, weight_ref, far_ref) = refs[:planes], refs[planes:]
    plane, core = own_plane(planes), own_core()
    for b in range(2 * planes):
        lanes = slice(b * ROWS, (b + 1) * ROWS)
        lane = block_lane(planes, b, plane, core)
        total = jnp.exp(pos_ref[:, lanes])
        for one in sums:
            total = total + one[:, pl.ds(lane, ROWS)]
        if b == 0:
            total_ref[...] = total
        weight_ref[:, lanes] = exp_ref[:, lanes] * (SCALE / total)
    far_ref[...] = weighted(planes, weight_ref, pick_ref, own_stack, other_stack, (3,)).astype(LOW)


def weighted(planes, weight_ref, pick_ref, own_stack, other_stack, slots):
    side = planes * ROWS
    below = lax.broadcasted_iota(jnp.int32, (ROWS, side), 0).astype(F32) + 1.0
    result = 0.0
    for at, stack in ((0, own_stack), (side, other_stack)):
        weights = weight_ref[:, at : at + side]
        high = weights.astype(LOW).astype(F32)
        for part in (high, weights - high):
            rows = [
                jnp.where(below == pick_ref[q : q + 1, at : at + side], part[q : q + 1, :], 0.0)
                for q in slots
            ]
            result = result + dot(jnp.concatenate(rows, axis=0).astype(LOW), stack[0:side, :])
    return result


def near_terms(planes, weight_ref, pick_ref, own_stack, other_stack, own_ref, x_ref, h_ref):
    result = weighted(planes, weight_ref, pick_ref, own_stack, other_stack, (0, 1, 2))
    own_ref[...] = result[0:ROWS, :]
    x_ref[...] = result[ROWS : 2 * ROWS, :].astype(LOW)
    h_ref[...] = result[2 * ROWS :, :]


def added(own_ref, other_ref, x_ref, out_ref, x_out):
    out_ref[...] = (own_ref[...] + other_ref[...].astype(F32)).astype(LOW)
    x_out[...] = x_ref[...]


def group_terms(*refs):
    nears, groups, (programs, traces, total_ref, trace_own) = refs[:2], refs[2:4], refs[4:8]
    prog_base, trace_base, prog_out, trace_out, size_ref, loss_ref = refs[8:]

    def part(which):
        at = [(x * 3 + which) * ROWS for x in range(2)]
        return jnp.concatenate([g[a : a + ROWS, :] for a in at for g in groups], axis=0)

    highs = [n[x * ROWS : (x + 1) * ROWS, :] for x in range(2) for n in nears]
    trace = (jnp.concatenate(highs, axis=0), part(0))
    prog = (part(1), part(2))
    scores = SCALE * dot3(prog, trace, (1, 1))
    exps = jnp.exp(scores)
    total = jnp.sum(exps, axis=1, keepdims=True)
    weights = exps / total
    prog_unit, prog_len = normalize(programs[...])
    trace_unit, trace_len = normalize(traces[...])
    prog_out[...] = prog_unit
    trace_out[...] = trace_unit
    pos = SCALE * jnp.sum(prog_unit * trace_unit, axis=-1, keepdims=True)
    hard_total = to_column(total_ref[...])
    pull = jnp.exp(pos) / hard_total - 2.0
    lane = lax.broadcasted_iota(jnp.int32, (ROWS, ROWS), 1)
    sizes = jnp.where(lane == 0, prog_len, jnp.where(lane == 1, trace_len, SCALE / hard_total))
    size_ref[...] = sizes
    group_prog = dot3(halves(weights[0:ROWS, :]), trace)
    prog_base[...] = SCALE * (group_prog + pull * trace_unit)
    group_trace = dot3(halves(jnp.transpose(weights[:, 0:ROWS])), prog)
    trace_base[...] = SCALE * (group_trace + pull * prog_unit) + trace_own[...]
    loss_ref[...] = to_row(jnp.log(total[0:ROWS, :]) - 2.0 * pos) + jnp.log(total_ref[...])


def finish(planes, prog_base, trace_base, prog_unit, trace_unit, size_ref, *refs):
    progs, traces, (prog_out, trace_out) = refs[:planes], refs[planes : planes + 2], refs[planes + 2 :]
    back = trace_base[...]
    for one in traces:
        back = back + one[...].astype(F32)
    hard = progs[0][...]
    for one in progs[1:]:
        hard = hard + one[...].astype(F32)
    direction = prog_base[...] + size_ref[:, 2:3] * hard
    for unit, towards, length, out in (
        (prog_unit[...], direction, size_ref[:, 0:1], prog_out),
        (trace_unit[...], back, size_ref[:, 1:2], trace_out),
    ):
        along = jnp.sum(unit * towards, axis=-1, keepdims=True)
        out[...] = (towards - unit * along) / length


def call(body, outs, flops, moved, scratch=(), in_specs=None, limit=VMEM_LIMIT):
    return pl.pallas_call(
        body,
        out_shape=[jax.ShapeDtypeStruct(shape, dtype) for shape, dtype in outs],
        scratch_shapes=list(scratch),
        **({"in_specs": in_specs} if in_specs else {}),
        compiler_params=pltpu.CompilerParams(vmem_limit_bytes=limit),
        cost_estimate=pl.CostEstimate(flops=flops, bytes_accessed=moved, transcendentals=0),
    )


def joined(own_ref, x_ref, _, out_ref):
    out_ref[0 : 3 * ROWS, :] = own_ref[...]
    out_ref[3 * ROWS :, :] = x_ref[...]


def on_device(dp_count, blk_count, programs, traces, hard_owner, hard_row):
    rows, feat = programs.shape
    planes = dp_count // 2
    size = dp_count * blk_count
    both = ("dp", "blk")

    def flipped(value, bits):
        return lax.ppermute(value, both, [(i, i ^ bits) for i in range(size)])

    def to_plane(value, k):
        return flipped(value, k * blk_count)

    x_bit, h_bit = 2, planes * blk_count
    block = rows * feat
    shape, side, width = (rows, feat), planes * rows, 2 * planes * rows
    hbm = pl.BlockSpec(memory_space=pltpu.HBM)
    index = hard_owner.shape[::-1]
    *sent, high = call(
        functools.partial(prepare, planes),
        [((rows + MORE, feat), LOW)] * planes + [(shape, LOW)],
        10 * block,
        20 * block,
        [
            pltpu.VMEM(shape, F32),
            pltpu.VMEM(shape, F32),
            pltpu.VMEM(index, jnp.int32),
            pltpu.VMEM(index, jnp.int32),
            pltpu.VMEM((8 * planes, rows), F32),
            pltpu.SemaphoreType.DMA((4,)),
        ],
        [hbm] * 4,
        None,
    )(programs, traces, hard_owner.T, hard_row.T)
    high_h = flipped(high, h_bit)
    far_first = list(range(planes - 1, 0, -1))
    arrived = [to_plane(sent[k], k) for k in far_first]
    stack = call(
        functools.partial(stack_programs, planes), [((side + 8 * planes, feat), LOW)], STACK, 0
    )(sent[0], *arrived)[0]
    high_h = call(stack_traces, [(shape, LOW)], HALF, 0)(high_h)[0]
    high_x, far = flipped(high, x_bit), flipped(high_h, x_bit)
    far = call(stack_traces, [(shape, LOW)], FAR, 0)(far)[0]
    near = call(stack_traces, [((3 * rows, feat), LOW)], TRACE, 0)(high, high_x, high_h)[0]
    group = call(group_parts, [((3 * rows, feat), LOW)], 10 * block, 20 * block)(
        programs, traces, high_h
    )[0]
    group_x = flipped(group, x_bit)
    other_stack, other_near, other_far = (flipped(one, 1) for one in (stack, near, far))
    stacks = stack, other_stack

    lists = [((8, width), F32), ((8, width), F32), ((1, width), F32)]
    exps, picks, pos = call(functools.partial(score_near, planes), lists, NEAR, 0)(
        *stacks, near, other_near
    )
    exps, sums = call(functools.partial(score_far, planes), lists[1:], LAST, 0)(
        exps, picks, *stacks, far, other_far
    )
    all_sums = [sums] + [to_plane(sums, k) for k in [2] + [k for k in far_first if k != 2]]

    mark, prog_own, *prog_parts = call(
        functools.partial(program_terms, planes),
        [((8, rows), F32), (shape, F32)] + [(shape, LOW)] * (planes - 1),
        AHEAD,
        0,
    )(exps, picks, near, far, other_near, other_far, sums)
    total, weights, part_xh = call(
        functools.partial(far_terms, planes), [((1, rows), F32), lists[0], (shape, LOW)], 0, 0
    )(exps, picks, pos, *stacks, mark, *all_sums)
    trace_own, part_x, part_h = call(
        functools.partial(near_terms, planes),
        [(shape, F32), (shape, LOW), (shape, F32)],
        12 * rows * width * feat,
        4 * width * feat,
    )(weights, picks, *stacks)
    for_h, part_x = call(added, [(shape, LOW)] * 2, block, 4 * block)(
        part_h, flipped(part_xh, x_bit), part_x
    )
    trace_back = [flipped(for_h, h_bit), flipped(part_x, x_bit)]

    groups = call(joined, [((6 * rows, feat), LOW)], JOIN, 0)(group, group_x, total)[0]
    prog_back = [to_plane(part, k) for k, part in enumerate(prog_parts, 1)]
    *bases, loss = call(
        group_terms,
        [(shape, F32)] * 4 + [((rows, rows), F32), ((1, rows), F32)],
        block,
        block,
    )(near, other_near, groups, flipped(groups, 1), programs, traces, total, trace_own)

    grad_programs, grad_traces = call(
        functools.partial(finish, planes), [(shape, F32)] * 2, block, block
    )(*bases, prog_own, *prog_back, *trace_back)
    return grad_programs, grad_traces, loss.reshape(rows)


def solution(mesh):
    spec = P(("dp", "blk"), None)
    return jax.shard_map(
        functools.partial(on_device, mesh.shape["dp"], mesh.shape["blk"]),
        mesh=mesh,
        in_specs=(spec,) * 4,
        out_specs=(spec, spec, P(("dp", "blk"))),
        check_vma=False,
    )
```
